256 devices in a mesh: group: 4 (over y_hi, core), dp: 64 (over z, y_lo, x).
Axes of the slice: x: 4, y: 4 (y_hi: 2, y_lo: 2; y = y_hi * 2 + y_lo), z: 8, core: 2. Of those that a mesh axis runs over, the one named last changes fastest.
Arguments:
- gelu_pooled_inner: bfloat16 [14336, 12288], P(('group', 'dp')), may hold values from -1.5 to 1.5
- frozen_pooled_trunk_result: bfloat16 [14336, 3072], P(('group', 'dp')), may hold values from -62 to 62
- narrowing_weight: bfloat16 [12288, 16], replicated, may hold values from -0.0546875 to 0.0546875
- widening_weight: bfloat16 [16, 3072], replicated, may hold values from -1.5 to 1.5
- closing_standardize_multiplier: float32 [3072], replicated, may hold values from 0.5 to 2
- closing_standardize_addend: float32 [3072], replicated, may hold values from -3 to 3
- closing_projection_weight: bfloat16 [3072, 1024], replicated, may hold values from -0.109375 to 0.109375
- sentence_encodings: bfloat16 [14336, 1024], P(('group', 'dp')), may hold values from -62 to 62
- logged_sharpening: float32 [1], replicated, may hold values from 2 to 2.6
- sigmoid_threshold_term: float32 [1], replicated, may hold values from -4 to -2
Outputs:
- sphere_visual_derivative: float32 [14336, 1024], P(('group', 'dp'))
- adapter_down_gradient: float32 [12288, 16], replicated
- adapter_up_gradient: float32 [16, 3072], replicated
The draws below stay inside these ranges and needn't reach their ends.
All inputs are finite; a program needn't handle non-finite values.
Results may differ from the reference program's by a relative error of at most 0.0085.
Values may be sent and summed in bfloat16 or wider, within the bound.
A program may use at most 128 MiB of HBM per device.

```python
import math
import jax
import jax.numpy as jnp
from jax import lax

E = 1024
TRAILING_DEPTH = 3072
INNER_WIDTH = 12288
LOWDIM_SIZE = 16
IMG_DEV = 56
BATCH = 14336
N_GROUP = 4


def spread_scales(key, row_count, col_count):
    col_key, row_key = jax.random.split(key, 2)
    col_scale = jnp.exp(jax.random.uniform(col_key, (1, col_count), jnp.float32, math.log(0.3), math.log(3.0)))
    row_scale = jnp.exp(jax.random.uniform(row_key, (row_count, 1), jnp.float32, math.log(0.5), math.log(5.0)))
    return col_scale * row_scale


def draw_frozen_pooled_trunk_result(key, part):
    key = jax.random.fold_in(key, 11)
    value_key, scale_key = jax.random.split(key, 2)
    values = jnp.clip(jax.random.normal(value_key, (BATCH, TRAILING_DEPTH), jnp.float32), -4.0, 4.0)
    return (values * spread_scales(scale_key, BATCH, TRAILING_DEPTH)).astype(jnp.bfloat16)


def draw_sentence_encodings(key, part):
    key = jax.random.fold_in(key, 23)
    value_key, scale_key = jax.random.split(key, 2)
    values = jnp.clip(jax.random.normal(value_key, (BATCH, E), jnp.float32), -4.0, 4.0)
    return (values * spread_scales(scale_key, BATCH, E)).astype(jnp.bfloat16)


def steps_of(own_key, dims, shards, low, high):
    def one(position, shards_of):
        heights = jax.random.uniform(jax.random.fold_in(jax.random.fold_in(own_key, 6), position), (shards_of,), jnp.float32, low / len(shards), high / len(shards))
        return jnp.repeat(jnp.exp(heights), dims[position] // shards_of).reshape((-1,) + (1,) * (len(dims) - position - 1))

    gain = one(*shards[0])
    for cut in shards[1:]:
        gain = gain * one(*cut)
    return gain


def bell_draw(own_key, shape, scale, limit, shards=(), held_as=jnp.bfloat16):
    drawn = jax.random.normal(own_key, shape, jnp.float32) * scale
    if len(shards) > 0:
        drawn = steps_of(own_key, shape, shards, -0.22, 0.18) * drawn
    return jnp.clip(drawn, min=-limit, max=limit).astype(held_as)


def setup_inputs(seed: int = 0) -> dict:
    keys = jax.random.split(jax.random.key(seed), 11)
    return {
        "gelu_pooled_inner": bell_draw(keys[0], (BATCH, INNER_WIDTH), 0.25, 1.5, ((0, 256),)),
        "frozen_pooled_trunk_result": draw_frozen_pooled_trunk_result(jax.random.fold_in(keys[10], 71), 0),
        "narrowing_weight": bell_draw(keys[2], (INNER_WIDTH, LOWDIM_SIZE), INNER_WIDTH ** -0.5, 0.0546875),
        "widening_weight": bell_draw(keys[3], (LOWDIM_SIZE, TRAILING_DEPTH), LOWDIM_SIZE ** -0.5, 1.5),
        "closing_standardize_multiplier": jnp.clip(jnp.exp(jax.random.uniform(keys[4], (TRAILING_DEPTH,), jnp.float32, math.log(0.5), math.log(2.0))), 0.5, 2.0),
        "closing_standardize_addend": bell_draw(keys[5], (TRAILING_DEPTH,), 0.5, 3.0, (), jnp.float32),
        "closing_projection_weight": bell_draw(keys[6], (TRAILING_DEPTH, E), TRAILING_DEPTH ** -0.5, 0.109375),
        "sentence_encodings": draw_sentence_encodings(jax.random.fold_in(keys[10], 71), 0),
        "logged_sharpening": jnp.clip(jax.random.uniform(keys[8], (1,), jnp.float32, 2.0, 2.6), 2.0, 2.6),
        "sigmoid_threshold_term": jnp.clip(jax.random.uniform(keys[9], (1,), jnp.float32, -4.0, -2.0), -4.0, -2.0),
    }


norm_eps = 1e-06

def visual_encoder_evaluate(gelu_pooled_inner, frozen_pooled_trunk_result, narrowing_weight, widening_weight, closing_standardize_multiplier, closing_standardize_addend, closing_projection_weight):
    lowdim_compressed = jnp.dot(gelu_pooled_inner, narrowing_weight, preferred_element_type=jnp.float32).astype(jnp.bfloat16)
    trailing_result = frozen_pooled_trunk_result.astype(jnp.float32) + jnp.dot(lowdim_compressed, widening_weight, preferred_element_type=jnp.float32)
    centred = trailing_result - lax.optimization_barrier(jnp.mean(trailing_result, axis=1, keepdims=True))
    reciprocal_spread = lax.rsqrt(lax.optimization_barrier(jnp.mean(centred * centred, axis=1, keepdims=True)) + norm_eps)
    standardized_traits = centred * reciprocal_spread
    head_in = (standardized_traits * closing_standardize_multiplier + closing_standardize_addend).astype(jnp.bfloat16)
    embedding = jnp.dot(head_in, closing_projection_weight, preferred_element_type=jnp.float32)
    reciprocal_magnitude = lax.rsqrt(lax.optimization_barrier(jnp.sum(embedding * embedding, axis=1, keepdims=True)) + norm_eps)
    return (lowdim_compressed, standardized_traits, reciprocal_spread, embedding * reciprocal_magnitude, reciprocal_magnitude)

def unit_rows(sentence_encodings):
    values = sentence_encodings.astype(jnp.float32)
    return (values * lax.rsqrt(lax.optimization_barrier(jnp.sum(values * values, axis=1, keepdims=True)) + norm_eps)).astype(jnp.bfloat16)

def reference(gelu_pooled_inner, frozen_pooled_trunk_result, narrowing_weight, widening_weight, closing_standardize_multiplier, closing_standardize_addend, closing_projection_weight, sentence_encodings, logged_sharpening, sigmoid_threshold_term):
    lowdim_compressed, standardized_traits, reciprocal_spread, sphere_visual, reciprocal_magnitude = visual_encoder_evaluate(gelu_pooled_inner, frozen_pooled_trunk_result, narrowing_weight, widening_weight, closing_standardize_multiplier, closing_standardize_addend, closing_projection_weight)
    photo_batch_part = sphere_visual.astype(jnp.bfloat16)
    text_rows = unit_rows(sentence_encodings)
    steepness_number = jnp.exp(logged_sharpening[0])
    beginning_position = sigmoid_threshold_term[0]
    block_rows = IMG_DEV * N_GROUP
    all_ids = jnp.arange(BATCH, dtype=jnp.int32)

    def block_grad(packed):
        image_block, block_ids = packed
        cosine_values = jnp.dot(image_block, text_rows.T, preferred_element_type=jnp.float32)
        affinity_entries = steepness_number * cosine_values + beginning_position
        positive_sign_targets = (block_ids[:, None] == all_ids[None, :]).astype(jnp.float32)
        penalty_coefficients = (steepness_number * (jax.nn.sigmoid(affinity_entries) - positive_sign_targets)).astype(jnp.bfloat16)
        return jnp.dot(penalty_coefficients, text_rows, preferred_element_type=jnp.float32)
    blocks = BATCH // block_rows
    sphere_visual_derivative = lax.map(block_grad, (photo_batch_part.reshape(blocks, block_rows, E), all_ids.reshape(blocks, block_rows))).reshape(BATCH, E)
    projection = lax.optimization_barrier(jnp.sum(sphere_visual * sphere_visual_derivative, axis=1, keepdims=True))
    embed_grad = (reciprocal_magnitude * (sphere_visual_derivative - sphere_visual * projection)).astype(jnp.bfloat16)
    head_grad = jnp.dot(embed_grad, closing_projection_weight.T, preferred_element_type=jnp.float32)
    scaled = head_grad * closing_standardize_multiplier
    trailing_derivative = reciprocal_spread * (scaled - lax.optimization_barrier(jnp.mean(scaled, axis=1, keepdims=True)) - standardized_traits * lax.optimization_barrier(jnp.mean(scaled * standardized_traits, axis=1, keepdims=True)))
    trailing_derivative = trailing_derivative.astype(jnp.bfloat16)
    adapter_up_gradient = jnp.dot(lowdim_compressed.T, trailing_derivative, preferred_element_type=jnp.float32)
    lowdim_reverse_pass = jnp.dot(trailing_derivative, widening_weight.T, preferred_element_type=jnp.float32).astype(jnp.bfloat16)
    adapter_down_gradient = jnp.dot(gelu_pooled_inner.T, lowdim_reverse_pass, preferred_element_type=jnp.float32)
    return (sphere_visual_derivative, adapter_down_gradient, adapter_up_gradient)
```

```python
import jax
import jax.numpy as jnp
from jax import lax
from jax.experimental import pallas as pl
from jax.experimental.pallas import tpu as pltpu
from jax.sharding import PartitionSpec as P

norm_eps = 1e-06
MESH = pl.DeviceIdType.MESH
BF16, F32 = jnp.bfloat16, jnp.float32

X, YL, YH, Z = 4, 2, 2, 8
Y = YL * YH
ROWS = 56
PAIR = 2 * ROWS
E, DEPTH, INNER, RANK = 1024, 3072, 12288, 16
QUARTER = E // 4
IMAGES = X * ROWS
TEXTS = Y * PAIR
PLANE = X * Y
CUT = 512
UP, DOWN = Z // 2, Z // 2 - 1


def remote(src, dst, send_sem, recv_sem, device):
    return pltpu.make_async_remote_copy(
        src_ref=src,
        dst_ref=dst,
        send_sem=send_sem,
        recv_sem=recv_sem,
        device_id=device,
        device_id_type=MESH,
    )


def nt(a, b):
    return lax.dot_general(a, b, (((1,), (1,)), ((), ())), preferred_element_type=F32)


def nn(a, b):
    return lax.dot_general(a, b, (((1,), (0,)), ((), ())), preferred_element_type=F32)


def kernel(
    inner_h,
    trunk_h,
    narrow_h,
    widen_h,
    gain_h,
    bias_h,
    head_h,
    text_h,
    sharp_ref,
    shift_ref,
    dv_h,
    grad_h,
    inner,
    trunk,
    narrow,
    widen,
    gain,
    bias,
    head,
    raw,
    texts,
    image_wire,
    images,
    dv,
    dv_send,
    dv_recv,
    dv_own,
    unit,
    normed,
    grads,
    pair_send,
    pair_recv,
    half,
    plane_send,
    plane_recv,
    ring_recv,
    final,
    load_sem,
    raw_send,
    raw_recv,
    pz_send,
    pz_recv,
    py_send,
    py_recv,
    qy_send,
    qy_recv,
    qz_send,
    qz_recv,
    sib_send,
    sib_recv,
    img_send,
    img_recv,
    rs_send,
    rs_recv,
    pair_ssem,
    pair_rsem,
    plane_ssem,
    plane_rsem,
    ring_ssem,
    ring_rsem,
    back_ssem,
    back_rsem,
    last_ssem,
    last_rsem,
    out_sem,
):
    g, d = lax.axis_index("group"), lax.axis_index("dp")
    c, yh = lax.rem(g, 2), lax.div(g, 2)
    z, yl, x = lax.div(d, YL * X), lax.rem(lax.div(d, X), YL), lax.rem(d, X)
    y = yh * YL + yl
    k = y * X + x

    def device(xx, yy, zz, cc):
        return (
            lax.div(yy, YL) * 2 + cc,
            zz * (YL * X) + lax.rem(yy, YL) * X + xx,
        )

    sibling = device(x, y, z, 1 - c)
    above = device(x, y, lax.rem(z + 1, Z), c)
    below = device(x, y, lax.rem(z + Z - 1, Z), c)

    def at_y(o):
        return lax.rem(y + o, Y)

    def at_x(o):
        return lax.rem(x + o, X)

    def at_z(o):
        return lax.rem(z + o + Z, Z)

    def at_k(o):
        return lax.rem(k + o, PLANE)

    def plane_device(kk):
        return device(lax.rem(kk, X), lax.div(kk, X), z, c)

    loads = [
        pltpu.make_async_copy(text_h, raw.at[c], load_sem.at[0]),
        pltpu.make_async_copy(inner_h, inner, load_sem.at[1]),
        pltpu.make_async_copy(narrow_h, narrow, load_sem.at[2]),
        pltpu.make_async_copy(widen_h, widen, load_sem.at[3]),
        pltpu.make_async_copy(trunk_h, trunk, load_sem.at[4]),
        pltpu.make_async_copy(gain_h, gain, load_sem.at[5]),
        pltpu.make_async_copy(bias_h, bias, load_sem.at[6]),
        pltpu.make_async_copy(head_h, head, load_sem.at[7]),
    ]
    barrier = pltpu.get_barrier_semaphore()
    pl.semaphore_signal(barrier, inc=1, device_id=sibling, device_id_type=MESH)

    @pl.loop(1, PLANE)
    def _(o):
        pl.semaphore_signal(barrier, inc=1, device_id=plane_device(at_k(o)), device_id_type=MESH)

    @pl.loop(1, Z)
    def _(o):
        pl.semaphore_signal(barrier, inc=1, device_id=device(x, y, at_z(o), c), device_id_type=MESH)

    for load in loads:
        load.start()
    pl.semaphore_wait(barrier, 1 + (PLANE - 1) + (Z - 1))

    raw_copy = remote(text_h, raw.at[c], raw_send, raw_recv, sibling)
    raw_copy.start()
    loads[0].wait()
    raw_copy.wait_recv()

    halves = []
    for i in range(2):
        whole = raw[i].astype(F32)
        scale = lax.rsqrt(jnp.sum(whole * whole, axis=1, keepdims=True) + norm_eps)
        part = raw[i, :, pl.ds(pl.multiple_of(c * (E // 2), E // 2), E // 2)].astype(F32)
        halves.append(part * scale)
    block = jnp.concatenate(halves, axis=0).astype(BF16)
    texts[c, z, 0, y] = block[:, :QUARTER]
    texts[c, z, 1, y] = block[:, QUARTER:]

    def piece0_up(zz, hop):
        ref = texts.at[c, zz, 0, y]
        return remote(ref, ref, pz_send.at[hop], pz_recv.at[zz], above)

    def piece0_down(zz, hop):
        ref = texts.at[c, zz, 0, y]
        return remote(ref, ref, pz_send.at[UP + hop], pz_recv.at[zz], below)

    def piece0_y(zz, o):
        ref = texts.at[c, zz, 0, y]
        return remote(ref, ref, py_send.at[zz, o - 1], py_recv.at[zz, y], device(x, at_y(o), z, c))

    def piece0_y_wait(zz, o):
        ref = texts.at[c, zz, 0, at_y(o)]
        remote(ref, ref, py_send.at[0, 0], py_recv.at[zz, at_y(o)], sibling).wait_recv()

    def piece1_y(o):
        ref = texts.at[c, z, 1, y]
        return remote(ref, ref, qy_send.at[o - 1], qy_recv.at[y], device(x, at_y(o), z, c))

    def piece1_y_wait(o):
        ref = texts.at[c, z, 1, at_y(o)]
        remote(ref, ref, qy_send.at[0], qy_recv.at[at_y(o)], sibling).wait_recv()

    def piece1_up(zz, hop):
        ref = texts.at[c, zz, 1]
        return remote(ref, ref, qz_send.at[hop], qz_recv.at[zz], above)

    def piece1_down(zz, hop):
        ref = texts.at[c, zz, 1]
        return remote(ref, ref, qz_send.at[UP + hop], qz_recv.at[zz], below)

    def across(zz):
        ref = texts.at[c, zz]
        return remote(ref, ref, sib_send.at[zz], sib_recv.at[zz], sibling)

    def spread0(zz):
        @pl.loop(1, Y)
        def _(o):
            piece0_y(zz, o).start()

    @pl.loop(1, Y)
    def _(o):
        piece1_y(o).start()

    piece0_up(z, 0).start()
    piece0_down(z, 0).start()
    spread0(z)

    def pass0(distance):
        zz = at_z(-distance)
        piece0_up(zz, 0).wait_recv()
        if distance < UP:
            piece0_up(zz, distance).start()
        spread0(zz)
        if distance <= DOWN:
            zz = at_z(distance)
            piece0_down(zz, 0).wait_recv()
            if distance < DOWN:
                piece0_down(zz, distance).start()
            spread0(zz)

    loads[1].wait()
    loads[2].wait()
    step = INNER // 4
    low = jnp.zeros((ROWS, RANK), F32)
    for i in range(4):
        cols = pl.ds(i * step, step)
        low = low + nt(inner[:, cols], narrow[:, cols])
    low = low.astype(BF16)

    @pl.loop(1, Y)
    def _(o):
        piece1_y_wait(o)

    piece1_up(z, 0).start()
    piece1_down(z, 0).start()
    pass0(1)

    loads[3].wait()
    loads[4].wait()
    loads[5].wait()
    loads[6].wait()
    section = trunk[...].astype(F32) + nn(low, widen[...])
    centred = section - jnp.mean(section, axis=1, keepdims=True)
    inv_std = lax.rsqrt(jnp.mean(centred * centred, axis=1, keepdims=True) + norm_eps)
    spread = centred * inv_std
    normed[...] = spread
    head_in = (spread * gain[...] + bias[...]).astype(BF16)
    pass0(2)
    loads[7].wait()
    embedding = nn(head_in, head[...])
    inv_len = lax.rsqrt(jnp.sum(embedding * embedding, axis=1, keepdims=True) + norm_eps)
    embedding = embedding * inv_len
    unit[...] = embedding

    def to_wire(ref, quarters):
        ref[:, :QUARTER] = jnp.concatenate([quarters[0], quarters[2]], axis=0).astype(BF16)
        ref[:, QUARTER:] = jnp.concatenate([quarters[1], quarters[3]], axis=0).astype(BF16)

    def from_wire(ref):
        left = ref[:, :QUARTER].astype(F32)
        right = ref[:, QUARTER:].astype(F32)
        return [left[:ROWS], right[:ROWS], left[ROWS:], right[ROWS:]]

    to_wire(image_wire.at[x], [embedding[:, q * QUARTER : (q + 1) * QUARTER] for q in range(4)])

    def send_images(o):
        ref = image_wire.at[x]
        return remote(ref, ref, img_send.at[o - 1], img_recv.at[x], device(at_x(o), y, z, c))

    @pl.loop(1, X)
    def _(o):
        send_images(o).start()

    pass0(3)
    pass0(4)

    def prepare(s):
        zz = at_z(lax.rem(s, 2) * -(lax.div(s + 1, 2)) + (1 - lax.rem(s, 2)) * lax.div(s, 2))

        @pl.when(lax.rem(s, 2) == 1)
        def _():
            distance = lax.div(s + 1, 2)
            piece1_up(zz, 0).wait_recv()

            @pl.when(distance < UP)
            def _():
                piece1_up(zz, distance).start()

        @pl.when((lax.rem(s, 2) == 0) & (s > 0))
        def _():
            distance = lax.div(s, 2)
            piece1_down(zz, 0).wait_recv()

            @pl.when(distance < DOWN)
            def _():
                piece1_down(zz, distance).start()

        @pl.loop(1, Y)
        def _(o):
            piece0_y_wait(zz, o)

        across(zz).start()

    prepare(jnp.int32(0))

    @pl.loop(1, X)
    def _(o):
        ref = image_wire.at[at_x(o)]
        remote(ref, ref, img_send.at[0], img_recv.at[at_x(o)], sibling).wait_recv()

    wires = [from_wire(image_wire.at[i]) for i in range(X)]
    for q in range(4):
        images[q] = jnp.concatenate([wire[q] for wire in wires], axis=0).astype(BF16)

    sharp = jnp.exp(jnp.full((1, TEXTS), sharp_ref[0], F32))
    shift = jnp.full((1, TEXTS), shift_ref[0], F32)

    dv[...] = jnp.zeros_like(dv)

    @pl.loop(0, Z)
    def _(s):
        @pl.when(s < Z - 1)
        def _():
            prepare(s + 1)

        zz = at_z(lax.rem(s, 2) * -(lax.div(s + 1, 2)) + (1 - lax.rem(s, 2)) * lax.div(s, 2))
        ref = texts.at[1 - c, zz]
        remote(ref, ref, sib_send.at[0], sib_recv.at[zz], sibling).wait_recv()
        parts = [texts[q // 2, zz, q % 2].reshape(TEXTS, QUARTER) for q in range(4)]
        cosine = nt(images[0], parts[0])
        for q in range(1, 4):
            cosine = cosine + nt(images[q], parts[q])
        row = lax.broadcasted_iota(jnp.int32, (IMAGES, TEXTS), 0) - x * ROWS
        col = lax.broadcasted_iota(jnp.int32, (IMAGES, TEXTS), 1) - y * PAIR - c * ROWS
        same = (row == col) & (row >= 0) & (row < ROWS) & (s == 0)
        weights = sharp * (jax.nn.sigmoid(sharp * cosine + shift) - jnp.where(same, 1.0, 0.0))
        weights = weights.astype(BF16)
        for q in range(4):
            dv[q] += nn(weights, parts[q])

    def send_sum(o):
        return remote(
            dv_send.at[o - 1],
            dv_recv.at[x],
            rs_send.at[o - 1],
            rs_recv.at[x],
            device(at_x(o), y, z, c),
        )

    def rows_of(xx):
        return pl.ds(pl.multiple_of(xx * ROWS, 8), ROWS)

    for o in range(1, X):
        to_wire(dv_send.at[o - 1], [dv[q, rows_of(at_x(o))] for q in range(4)])
        send_sum(o).start()
    total = [dv[q, rows_of(x)] for q in range(4)]
    for o in range(1, X):
        ref = dv_recv.at[at_x(o)]
        remote(ref, ref, rs_send.at[0], rs_recv.at[at_x(o)], sibling).wait_recv()
        total = [a + b for a, b in zip(total, from_wire(ref))]
    derivative = jnp.concatenate(total, axis=1)
    dv_own[...] = derivative
    dv_copy = pltpu.make_async_copy(dv_own, dv_h, out_sem.at[0])
    dv_copy.start()

    embedding = unit[...]
    along = jnp.sum(embedding * derivative, axis=1, keepdims=True)
    embed_grad = (inv_len * (derivative - embedding * along)).astype(BF16)
    scaled = nt(embed_grad, head[...]) * gain[...]
    spread = normed[...]
    section_grad = inv_std * (
        scaled
        - jnp.mean(scaled, axis=1, keepdims=True)
        - spread * jnp.mean(scaled * spread, axis=1, keepdims=True)
    )
    section_grad = section_grad.astype(BF16)
    back = nt(widen[...], section_grad).astype(BF16)
    up = lax.dot_general(low, section_grad, (((0,), (0,)), ((), ())), preferred_element_type=F32)
    n_down, n_up = INNER // CUT, DEPTH // CUT
    for i in range(n_down):
        grads[i // PLANE, i % PLANE] = nn(back, inner[:, pl.ds(i * CUT, CUT)])
    for i in range(n_up):
        j = n_down + i
        grads[j // PLANE, j % PLANE] = up[:, i * CUT : (i + 1) * CUT]
    for j in range(n_down + n_up, 2 * PLANE):
        grads[j // PLANE, j % PLANE] = jnp.zeros((RANK, CUT), F32)

    pair_send[...] = grads[1 - c].astype(BF16)
    pair_copy = remote(pair_send, pair_recv, pair_ssem, pair_rsem, sibling)
    pair_copy.start()
    pair_copy.wait_recv()
    half[...] = grads[c] + pair_recv[...].astype(F32)
    plane_send[...] = half[...].astype(BF16)

    def plane_copy(o):
        kk = at_k(o)
        return remote(
            plane_send.at[kk],
            plane_recv.at[k],
            plane_ssem.at[o - 1],
            plane_rsem.at[k],
            plane_device(kk),
        )

    @pl.loop(1, PLANE)
    def _(o):
        plane_copy(o).start()

    plane_recv[k] = plane_send[k]

    @pl.loop(1, PLANE)
    def _(o):
        ref = plane_recv.at[at_k(o)]
        remote(ref, ref, plane_ssem.at[0], plane_rsem.at[at_k(o)], sibling).wait_recv()

    ring_recv[z] = jnp.sum(plane_recv[...].astype(F32), axis=0).astype(BF16)

    def ring_copy(o):
        ref = ring_recv.at[z]
        return remote(ref, ref, ring_ssem.at[o - 1], ring_rsem.at[z], device(x, y, at_z(o), c))

    @pl.loop(1, Z)
    def _(o):
        ring_copy(o).start()

    @pl.loop(1, Z)
    def _(o):
        ref = ring_recv.at[at_z(o)]
        remote(ref, ref, ring_ssem.at[0], ring_rsem.at[at_z(o)], sibling).wait_recv()

    final[c, k] = jnp.sum(ring_recv[...].astype(F32), axis=0).astype(BF16)

    def back_copy(o):
        ref = final.at[c, k]
        return remote(ref, ref, back_ssem.at[o - 1], back_rsem.at[k], plane_device(at_k(o)))

    def last_copy(kk):
        ref = final.at[c, kk]
        return remote(ref, ref, last_ssem.at[kk], last_rsem.at[kk], sibling)

    @pl.loop(1, PLANE)
    def _(o):
        back_copy(o).start()

    last_copy(k).start()

    @pl.loop(1, PLANE)
    def _(o):
        kk = at_k(o)
        ref = final.at[c, kk]
        remote(ref, ref, back_ssem.at[0], back_rsem.at[kk], sibling).wait_recv()
        last_copy(kk).start()

    @pl.loop(0, PLANE)
    def _(kk):
        ref = final.at[1 - c, kk]
        remote(ref, ref, last_ssem.at[0], last_rsem.at[kk], sibling).wait_recv()

    grad_copy = pltpu.make_async_copy(final, grad_h, out_sem.at[1])
    grad_copy.start()

    raw_copy.wait_send()
    for hop in range(UP):
        piece0_up(z, hop).wait_send()
        piece1_up(z, hop).wait_send()
    for hop in range(DOWN):
        piece0_down(z, hop).wait_send()
        piece1_down(z, hop).wait_send()

    @pl.loop(1, Y)
    def _(o):
        piece1_y(o).wait_send()

        @pl.loop(0, Z)
        def _(zz):
            piece0_y(zz, o).wait_send()

    @pl.loop(0, Z)
    def _(zz):
        across(zz).wait_send()

    @pl.loop(1, X)
    def _(o):
        send_images(o).wait_send()
        send_sum(o).wait_send()

    pair_copy.wait_send()

    @pl.loop(1, PLANE)
    def _(o):
        plane_copy(o).wait_send()
        back_copy(o).wait_send()

    @pl.loop(1, Z)
    def _(o):
        ring_copy(o).wait_send()

    @pl.loop(0, PLANE)
    def _(kk):
        last_copy(kk).wait_send()

    dv_copy.wait()
    grad_copy.wait()


def body(
    gelu_pooled_inner,
    frozen_pooled_trunk_result,
    narrowing_weight,
    widening_weight,
    closing_standardize_multiplier,
    closing_standardize_addend,
    closing_projection_weight,
    sentence_encodings,
    logged_sharpening,
    sigmoid_threshold_term,
):
    anywhere = pl.BlockSpec(memory_space=pl.ANY)
    scalar = pl.BlockSpec(memory_space=pltpu.SMEM)
    dma = pltpu.SemaphoreType.DMA
    derivative, final = pl.pallas_call(
        kernel,
        out_shape=(
            jax.ShapeDtypeStruct((ROWS, E), F32),
            jax.ShapeDtypeStruct((2, PLANE, RANK, CUT), BF16),
        ),
        in_specs=[anywhere] * 8 + [scalar] * 2,
        out_specs=(anywhere, anywhere),
        scratch_shapes=[
            pltpu.VMEM((ROWS, INNER), BF16),
            pltpu.VMEM((ROWS, DEPTH), BF16),
            pltpu.VMEM((RANK, INNER), BF16),
            pltpu.VMEM((RANK, DEPTH), BF16),
            pltpu.VMEM((1, DEPTH), F32),
            pltpu.VMEM((1, DEPTH), F32),
            pltpu.VMEM((DEPTH, E), BF16),
            pltpu.VMEM((2, ROWS, E), BF16),
            pltpu.VMEM((2, Z, 2, Y, PAIR, QUARTER), BF16),
            pltpu.VMEM((X, PAIR, E // 2), BF16),
            pltpu.VMEM((4, IMAGES, QUARTER), BF16),
            pltpu.VMEM((4, IMAGES, QUARTER), F32),
            pltpu.VMEM((X - 1, PAIR, E // 2), BF16),
            pltpu.VMEM((X, PAIR, E // 2), BF16),
            pltpu.VMEM((ROWS, E), F32),
            pltpu.VMEM((ROWS, E), F32),
            pltpu.VMEM((ROWS, DEPTH), F32),
            pltpu.VMEM((2, PLANE, RANK, CUT), F32),
            pltpu.VMEM((PLANE, RANK, CUT), BF16),
            pltpu.VMEM((PLANE, RANK, CUT), BF16),
            pltpu.VMEM((PLANE, RANK, CUT), F32),
            pltpu.VMEM((PLANE, RANK, CUT), BF16),
            pltpu.VMEM((PLANE, RANK, CUT), BF16),
            pltpu.VMEM((Z, RANK, CUT), BF16),
            pltpu.VMEM((2, PLANE, RANK, CUT), BF16),
            dma((8,)),
            dma,
            dma,
            dma((UP + DOWN,)),
            dma((Z,)),
            dma((Z, Y - 1)),
            dma((Z, Y)),
            dma((Y - 1,)),
            dma((Y,)),
            dma((UP + DOWN,)),
            dma((Z,)),
            dma((Z,)),
            dma((Z,)),
            dma((X - 1,)),
            dma((X,)),
            dma((X - 1,)),
            dma((X,)),
            dma,
            dma,
            dma((PLANE - 1,)),
            dma((PLANE,)),
            dma((Z - 1,)),
            dma((Z,)),
            dma((PLANE - 1,)),
            dma((PLANE,)),
            dma((PLANE,)),
            dma((PLANE,)),
            dma((2,)),
        ],
        compiler_params=pltpu.CompilerParams(
            collective_id=0, has_side_effects=True, vmem_limit_bytes=48 * 1024 * 1024
        ),
    )(
        gelu_pooled_inner,
        frozen_pooled_trunk_result,
        narrowing_weight.T,
        widening_weight,
        closing_standardize_multiplier.reshape(1, DEPTH),
        closing_standardize_addend.reshape(1, DEPTH),
        closing_projection_weight,
        sentence_encodings,
        logged_sharpening,
        sigmoid_threshold_term,
    )
    pieces = final.reshape(2 * PLANE, RANK, CUT).transpose(1, 0, 2).reshape(RANK, -1).astype(F32)
    return derivative, pieces[:, :INNER].T, pieces[:, INNER : INNER + DEPTH]


def solution(mesh):
    rows = P(("group", "dp"), None)
    return jax.shard_map(
        body,
        mesh=mesh,
        in_specs=(rows, rows, P(), P(), P(), P(), P(), rows, P(), P()),
        out_specs=(rows, P(), P()),
        check_vma=False,
    )
```

```python
import jax
import jax.numpy as jnp
from jax import lax
from jax.experimental import pallas as pl
from jax.experimental.pallas import tpu as pltpu
from jax.sharding import PartitionSpec as P

norm_eps = 1e-06
MESH = pl.DeviceIdType.MESH
BF16, F32 = jnp.bfloat16, jnp.float32

X, YL, YH, Z = 4, 2, 2, 8
Y = YL * YH
ROWS = 56
PAIR = 2 * ROWS
E, DEPTH, INNER, RANK = 1024, 3072, 12288, 16
QUARTER = E // 4
IMAGES = X * ROWS
TEXTS = Y * PAIR
PLANE = X * Y
CUT = 512
UP, DOWN = Z // 2, Z // 2 - 1


def remote(src, dst, send_sem, recv_sem, device):
    return pltpu.make_async_remote_copy(
        src_ref=src,
        dst_ref=dst,
        send_sem=send_sem,
        recv_sem=recv_sem,
        device_id=device,
        device_id_type=MESH,
    )


def nt(a, b):
    return lax.dot_general(a, b, (((1,), (1,)), ((), ())), preferred_element_type=F32)


def nn(a, b):
    return lax.dot_general(a, b, (((1,), (0,)), ((), ())), preferred_element_type=F32)


def kernel(
    inner_h,
    trunk_h,
    narrow_h,
    widen_h,
    gain_h,
    bias_h,
    head_h,
    text_h,
    sharp_ref,
    shift_ref,
    dv_h,
    grad_h,
    inner,
    trunk,
    narrow,
    widen,
    gain,
    bias,
    head,
    raw,
    texts,
    image_wire,
    images,
    dv,
    dv_send,
    dv_recv,
    dv_own,
    unit,
    normed,
    grads,
    pair_send,
    pair_recv,
    half,
    plane_send,
    plane_recv,
    ring_recv,
    final,
    load_sem,
    raw_send,
    raw_recv,
    pz_send,
    pz_recv,
    py_send,
    py_recv,
    qy_send,
    qy_recv,
    qz_send,
    qz_recv,
    sib_send,
    sib_recv,
    img_send,
    img_recv,
    rs_send,
    rs_recv,
    pair_ssem,
    pair_rsem,
    plane_ssem,
    plane_rsem,
    ring_ssem,
    ring_rsem,
    back_ssem,
    back_rsem,
    last_ssem,
    last_rsem,
    out_sem,
):
    g, d = lax.axis_index("group"), lax.axis_index("dp")
    c, yh = lax.rem(g, 2), lax.div(g, 2)
    z, yl, x = lax.div(d, YL * X), lax.rem(lax.div(d, X), YL), lax.rem(d, X)
    y = yh * YL + yl
    k = y * X + x

    def device(xx, yy, zz, cc):
        return (
            lax.div(yy, YL) * 2 + cc,
            zz * (YL * X) + lax.rem(yy, YL) * X + xx,
        )

    sibling = device(x, y, z, 1 - c)
    above = device(x, y, lax.rem(z + 1, Z), c)
    below = device(x, y, lax.rem(z + Z - 1, Z), c)

    def at_y(o):
        return lax.rem(y + o, Y)

    def at_x(o):
        return lax.rem(x + o, X)

    def at_z(o):
        return lax.rem(z + o + Z, Z)

    def at_k(o):
        return lax.rem(k + o, PLANE)

    def plane_device(kk):
        return device(lax.rem(kk, X), lax.div(kk, X), z, c)

    loads = [
        pltpu.make_async_copy(text_h, raw.at[c], load_sem.at[0]),
        pltpu.make_async_copy(inner_h, inner, load_sem.at[1]),
        pltpu.make_async_copy(narrow_h, narrow, load_sem.at[2]),
        pltpu.make_async_copy(widen_h, widen, load_sem.at[3]),
        pltpu.make_async_copy(trunk_h, trunk, load_sem.at[4]),
        pltpu.make_async_copy(gain_h, gain, load_sem.at[5]),
        pltpu.make_async_copy(bias_h, bias, load_sem.at[6]),
        pltpu.make_async_copy(head_h, head, load_sem.at[7]),
    ]
    barrier = pltpu.get_barrier_semaphore()
    pl.semaphore_signal(barrier, inc=1, device_id=sibling, device_id_type=MESH)

    for neighbour in (above, below):
        pl.semaphore_signal(barrier, inc=1, device_id=neighbour, device_id_type=MESH)
    for o in range(1, Y):
        pl.semaphore_signal(
            barrier, inc=1, device_id=device(x, at_y(o), z, c), device_id_type=MESH
        )
    for o in range(1, X):
        pl.semaphore_signal(
            barrier, inc=1, device_id=device(at_x(o), y, z, c), device_id_type=MESH
        )

    for load in loads:
        load.start()
    pl.semaphore_wait(barrier, 1 + 2 + (Y - 1) + (X - 1))

    raw_copy = remote(text_h, raw.at[c], raw_send, raw_recv, sibling)
    raw_copy.start()
    pending = [raw_copy.wait_send]
    loads[0].wait()
    raw_copy.wait_recv()

    halves = []
    for i in range(2):
        whole = raw[i].astype(F32)
        scale = lax.rsqrt(jnp.sum(whole * whole, axis=1, keepdims=True) + norm_eps)
        part = raw[i, :, pl.ds(pl.multiple_of(c * (E // 2), E // 2), E // 2)].astype(F32)
        halves.append(part * scale)
    block = jnp.concatenate(halves, axis=0).astype(BF16)
    texts[c, z, 0, y] = block[:, :QUARTER]
    texts[c, z, 1, y] = block[:, QUARTER:]

    def piece0_up(zz, hop):
        ref = texts.at[c, zz, 0, y]
        return remote(ref, ref, pz_send.at[hop], pz_recv.at[zz], above)

    def piece0_down(zz, hop):
        ref = texts.at[c, zz, 0, y]
        return remote(ref, ref, pz_send.at[UP + hop], pz_recv.at[zz], below)

    def piece0_y(zz, o):
        ref = texts.at[c, zz, 0, y]
        return remote(ref, ref, py_send.at[zz, o - 1], py_recv.at[zz, y], device(x, at_y(o), z, c))

    def piece0_y_wait(zz, o):
        ref = texts.at[c, zz, 0, at_y(o)]
        remote(ref, ref, py_send.at[0, 0], py_recv.at[zz, at_y(o)], sibling).wait_recv()

    def piece1_y(o):
        ref = texts.at[c, z, 1, y]
        return remote(ref, ref, qy_send.at[o - 1], qy_recv.at[y], device(x, at_y(o), z, c))

    def piece1_y_wait(o):
        ref = texts.at[c, z, 1, at_y(o)]
        remote(ref, ref, qy_send.at[0], qy_recv.at[at_y(o)], sibling).wait_recv()

    def piece1_up(zz, o, hop):
        ref = texts.at[c, zz, 1, at_y(o)]
        return remote(ref, ref, qz_send.at[hop, o], qz_recv.at[zz, at_y(o)], above)

    def piece1_down(zz, o, hop):
        ref = texts.at[c, zz, 1, at_y(o)]
        return remote(ref, ref, qz_send.at[UP + hop, o], qz_recv.at[zz, at_y(o)], below)

    def across(zz):
        ref = texts.at[c, zz]
        return remote(ref, ref, sib_send.at[zz], sib_recv.at[zz], sibling)

    def spread0(zz):
        @pl.loop(1, Y)
        def _(o):
            piece0_y(zz, o).start()

    piece0_up(z, 0).start()
    piece0_down(z, 0).start()

    @pl.loop(1, Y)
    def _(o):
        piece1_y(o).start()

    piece1_up(z, 0, 0).start()
    piece1_down(z, 0, 0).start()
    spread0(z)

    def wait_piece0():
        for hop in range(UP):
            piece0_up(z, hop).wait_send()
        for hop in range(DOWN):
            piece0_down(z, hop).wait_send()

        @pl.loop(1, Y)
        def _(o):
            @pl.loop(0, Z)
            def _(zz):
                piece0_y(zz, o).wait_send()

    def wait_piece1():
        @pl.loop(0, Y)
        def _(o):
            for hop in range(UP):
                piece1_up(z, o, hop).wait_send()
            for hop in range(DOWN):
                piece1_down(z, o, hop).wait_send()

        @pl.loop(1, Y)
        def _(o):
            piece1_y(o).wait_send()

        @pl.loop(0, Z)
        def _(zz):
            across(zz).wait_send()

    pending += [wait_piece0, wait_piece1]

    def pass0(distance):
        zz = at_z(-distance)
        piece0_up(zz, 0).wait_recv()
        if distance < UP:
            piece0_up(zz, distance).start()
        spread0(zz)
        if distance <= DOWN:
            zz = at_z(distance)
            piece0_down(zz, 0).wait_recv()
            if distance < DOWN:
                piece0_down(zz, distance).start()
            spread0(zz)

    def pass1(distance, first, last):
        @pl.loop(first, last)
        def _(o):
            zz = at_z(-distance)
            piece1_up(zz, o, 0).wait_recv()
            if distance < UP:
                piece1_up(zz, o, distance).start()
            if distance <= DOWN:
                zz = at_z(distance)
                piece1_down(zz, o, 0).wait_recv()
                if distance < DOWN:
                    piece1_down(zz, o, distance).start()

    loads[1].wait()
    loads[2].wait()
    step = INNER // 4
    low = jnp.zeros((ROWS, RANK), F32)
    for i in range(4):
        cols = pl.ds(i * step, step)
        low = low + nt(inner[:, cols], narrow[:, cols])
    low = low.astype(BF16)

    pass0(1)
    pass1(1, 0, 1)

    @pl.loop(1, Y)
    def _(o):
        piece1_y_wait(o)
        piece1_up(z, o, 0).start()
        piece1_down(z, o, 0).start()

    loads[3].wait()
    loads[4].wait()
    loads[5].wait()
    loads[6].wait()
    section = trunk[...].astype(F32) + nn(low, widen[...])
    centred = section - jnp.mean(section, axis=1, keepdims=True)
    inv_std = lax.rsqrt(jnp.mean(centred * centred, axis=1, keepdims=True) + norm_eps)
    spread = centred * inv_std
    normed[...] = spread
    head_in = (spread * gain[...] + bias[...]).astype(BF16)
    pass0(2)
    pass1(2, 0, 1)
    pass1(1, 1, Y)
    loads[7].wait()
    embedding = nn(head_in, head[...])
    inv_len = lax.rsqrt(jnp.sum(embedding * embedding, axis=1, keepdims=True) + norm_eps)
    embedding = embedding * inv_len
    unit[...] = embedding

    def to_wire(ref, quarters):
        ref[:, :QUARTER] = jnp.concatenate([quarters[0], quarters[2]], axis=0).astype(BF16)
        ref[:, QUARTER:] = jnp.concatenate([quarters[1], quarters[3]], axis=0).astype(BF16)

    def from_wire(ref):
        left = ref[:, :QUARTER].astype(F32)
        right = ref[:, QUARTER:].astype(F32)
        return [left[:ROWS], right[:ROWS], left[ROWS:], right[ROWS:]]

    to_wire(image_wire.at[x], [embedding[:, q * QUARTER : (q + 1) * QUARTER] for q in range(4)])

    def send_images(o):
        ref = image_wire.at[x]
        return remote(ref, ref, img_send.at[o - 1], img_recv.at[x], device(at_x(o), y, z, c))

    @pl.loop(1, X)
    def _(o):
        send_images(o).start()

    @pending.append
    def _():
        @pl.loop(1, X)
        def _(o):
            send_images(o).wait_send()

    pass0(3)
    pass1(3, 0, 1)
    pass1(2, 1, Y)

    def place(s):
        odd = lax.rem(s, 2)
        return at_z((1 - odd) * lax.div(s, 2) - odd * lax.div(s + 1, 2))

    def prepare(s):
        zz = place(s)

        @pl.loop(1, Y)
        def _(o):
            piece0_y_wait(zz, o)

        across(zz).start()

    prepare(jnp.int32(0))
    pass0(4)
    pass1(4, 0, 1)

    @pl.loop(1, X)
    def _(o):
        ref = image_wire.at[at_x(o)]
        remote(ref, ref, img_send.at[0], img_recv.at[at_x(o)], sibling).wait_recv()

    wires = [from_wire(image_wire.at[i]) for i in range(X)]
    for q in range(4):
        images[q] = jnp.concatenate([wire[q] for wire in wires], axis=0).astype(BF16)

    sharp = jnp.exp(jnp.full((1, TEXTS), sharp_ref[0], F32))
    shift = jnp.full((1, TEXTS), shift_ref[0], F32)

    dv[...] = jnp.zeros_like(dv)

    @pl.loop(0, Z)
    def _(s):
        @pl.when(s == 3)
        def _():
            pass1(3, 1, Y)

        @pl.when(s == 6)
        def _():
            pass1(4, 1, Y)

        @pl.when(s < Z - 1)
        def _():
            prepare(s + 1)

        zz = place(s)
        ref = texts.at[1 - c, zz]
        remote(ref, ref, sib_send.at[0], sib_recv.at[zz], sibling).wait_recv()
        parts = [texts[q // 2, zz, q % 2].reshape(TEXTS, QUARTER) for q in range(4)]
        cosine = nt(images[0], parts[0])
        for q in range(1, 4):
            cosine = cosine + nt(images[q], parts[q])
        row = lax.broadcasted_iota(jnp.int32, (IMAGES, TEXTS), 0) - x * ROWS
        col = lax.broadcasted_iota(jnp.int32, (IMAGES, TEXTS), 1) - y * PAIR - c * ROWS
        same = (row == col) & (row >= 0) & (row < ROWS) & (s == 0)
        weights = sharp * (jax.nn.sigmoid(sharp * cosine + shift) - jnp.where(same, 1.0, 0.0))
        weights = weights.astype(BF16)
        for q in range(4):
            dv[q] += nn(weights, parts[q])

    def send_sum(o):
        return remote(
            dv_send.at[o - 1],
            dv_recv.at[x],
            rs_send.at[o - 1],
            rs_recv.at[x],
            device(at_x(o), y, z, c),
        )

    def rows_of(xx):
        return pl.ds(pl.multiple_of(xx * ROWS, 8), ROWS)

    for o in range(1, X):
        to_wire(dv_send.at[o - 1], [dv[q, rows_of(at_x(o))] for q in range(4)])
        send_sum(o).start()

    @pending.append
    def _():
        @pl.loop(1, X)
        def _(o):
            send_sum(o).wait_send()
    total = [dv[q, rows_of(x)] for q in range(4)]
    for o in range(1, X):
        ref = dv_recv.at[at_x(o)]
        remote(ref, ref, rs_send.at[0], rs_recv.at[at_x(o)], sibling).wait_recv()
        total = [a + b for a, b in zip(total, from_wire(ref))]
    derivative = jnp.concatenate(total, axis=1)
    dv_own[...] = derivative
    dv_copy = pltpu.make_async_copy(dv_own, dv_h, out_sem.at[0])
    dv_copy.start()
    pending.append(dv_copy.wait)

    embedding = unit[...]
    along = jnp.sum(embedding * derivative, axis=1, keepdims=True)
    embed_grad = (inv_len * (derivative - embedding * along)).astype(BF16)
    scaled = nt(embed_grad, head[...]) * gain[...]
    spread = normed[...]
    section_grad = inv_std * (
        scaled
        - jnp.mean(scaled, axis=1, keepdims=True)
        - spread * jnp.mean(scaled * spread, axis=1, keepdims=True)
    )
    section_grad = section_grad.astype(BF16)
    back = nt(widen[...], section_grad).astype(BF16)
    up = lax.dot_general(low, section_grad, (((0,), (0,)), ((), ())), preferred_element_type=F32)
    n_down, n_up = INNER // CUT, DEPTH // CUT
    for i in range(n_down):
        grads[i // PLANE, i % PLANE] = nn(back, inner[:, pl.ds(i * CUT, CUT)])
    for i in range(n_up):
        j = n_down + i
        grads[j // PLANE, j % PLANE] = up[:, i * CUT : (i + 1) * CUT]
    for j in range(n_down + n_up, 2 * PLANE):
        grads[j // PLANE, j % PLANE] = jnp.zeros((RANK, CUT), F32)

    pair_send[...] = grads[1 - c].astype(BF16)
    pair_copy = remote(pair_send, pair_recv, pair_ssem, pair_rsem, sibling)
    pair_copy.start()
    pending.append(pair_copy.wait_send)
    pair_copy.wait_recv()
    half[...] = grads[c] + pair_recv[...].astype(F32)
    plane_send[...] = half[...].astype(BF16)

    def plane_copy(o):
        kk = at_k(o)
        return remote(
            plane_send.at[kk],
            plane_recv.at[k],
            plane_ssem.at[o - 1],
            plane_rsem.at[k],
            plane_device(kk),
        )

    @pl.loop(1, PLANE)
    def _(o):
        plane_copy(o).start()

    @pending.append
    def _():
        @pl.loop(1, PLANE)
        def _(o):
            plane_copy(o).wait_send()

    plane_recv[k] = plane_send[k]

    @pl.loop(1, PLANE)
    def _(o):
        ref = plane_recv.at[at_k(o)]
        remote(ref, ref, plane_ssem.at[0], plane_rsem.at[at_k(o)], sibling).wait_recv()

    ring_recv[z] = jnp.sum(plane_recv[...].astype(F32), axis=0).astype(BF16)

    def ring_copy(o):
        ref = ring_recv.at[z]
        return remote(ref, ref, ring_ssem.at[o - 1], ring_rsem.at[z], device(x, y, at_z(o), c))

    @pl.loop(1, Z)
    def _(o):
        ring_copy(o).start()

    @pending.append
    def _():
        @pl.loop(1, Z)
        def _(o):
            ring_copy(o).wait_send()

    @pl.loop(1, Z)
    def _(o):
        ref = ring_recv.at[at_z(o)]
        remote(ref, ref, ring_ssem.at[0], ring_rsem.at[at_z(o)], sibling).wait_recv()

    final[c, k] = jnp.sum(ring_recv[...].astype(F32), axis=0).astype(BF16)

    def back_copy(o):
        ref = final.at[c, k]
        return remote(ref, ref, back_ssem.at[o - 1], back_rsem.at[k], plane_device(at_k(o)))

    def last_copy(kk):
        ref = final.at[c, kk]
        return remote(ref, ref, last_ssem.at[kk], last_rsem.at[kk], sibling)

    @pl.loop(1, PLANE)
    def _(o):
        back_copy(o).start()

    @pending.append
    def _():
        @pl.loop(1, PLANE)
        def _(o):
            back_copy(o).wait_send()

    last_copy(k).start()

    @pending.append
    def _():
        @pl.loop(0, PLANE)
        def _(kk):
            last_copy(kk).wait_send()

    @pl.loop(1, PLANE)
    def _(o):
        kk = at_k(o)
        ref = final.at[c, kk]
        remote(ref, ref, back_ssem.at[0], back_rsem.at[kk], sibling).wait_recv()
        last_copy(kk).start()

    @pl.loop(0, PLANE)
    def _(kk):
        ref = final.at[1 - c, kk]
        remote(ref, ref, last_ssem.at[0], last_rsem.at[kk], sibling).wait_recv()

    grad_copy = pltpu.make_async_copy(final, grad_h, out_sem.at[1])
    grad_copy.start()
    pending.append(grad_copy.wait)

    for wait in pending:
        wait()


def body(
    gelu_pooled_inner,
    frozen_pooled_trunk_result,
    narrowing_weight,
    widening_weight,
    closing_standardize_multiplier,
    closing_standardize_addend,
    closing_projection_weight,
    sentence_encodings,
    logged_sharpening,
    sigmoid_threshold_term,
):
    anywhere = pl.BlockSpec(memory_space=pl.ANY)
    scalar = pl.BlockSpec(memory_space=pltpu.SMEM)
    dma = pltpu.SemaphoreType.DMA
    derivative, final = pl.pallas_call(
        kernel,
        out_shape=(
            jax.ShapeDtypeStruct((ROWS, E), F32),
            jax.ShapeDtypeStruct((2, PLANE, RANK, CUT), BF16),
        ),
        in_specs=[anywhere] * 8 + [scalar] * 2,
        out_specs=(anywhere, anywhere),
        scratch_shapes=[
            pltpu.VMEM((ROWS, INNER), BF16),
            pltpu.VMEM((ROWS, DEPTH), BF16),
            pltpu.VMEM((RANK, INNER), BF16),
            pltpu.VMEM((RANK, DEPTH), BF16),
            pltpu.VMEM((1, DEPTH), F32),
            pltpu.VMEM((1, DEPTH), F32),
            pltpu.VMEM((DEPTH, E), BF16),
            pltpu.VMEM((2, ROWS, E), BF16),
            pltpu.VMEM((2, Z, 2, Y, PAIR, QUARTER), BF16),
            pltpu.VMEM((X, PAIR, E // 2), BF16),
            pltpu.VMEM((4, IMAGES, QUARTER), BF16),
            pltpu.VMEM((4, IMAGES, QUARTER), F32),
            pltpu.VMEM((X - 1, PAIR, E // 2), BF16),
            pltpu.VMEM((X, PAIR, E // 2), BF16),
            pltpu.VMEM((ROWS, E), F32),
            pltpu.VMEM((ROWS, E), F32),
            pltpu.VMEM((ROWS, DEPTH), F32),
            pltpu.VMEM((2, PLANE, RANK, CUT), F32),
            pltpu.VMEM((PLANE, RANK, CUT), BF16),
            pltpu.VMEM((PLANE, RANK, CUT), BF16),
            pltpu.VMEM((PLANE, RANK, CUT), F32),
            pltpu.VMEM((PLANE, RANK, CUT), BF16),
            pltpu.VMEM((PLANE, RANK, CUT), BF16),
            pltpu.VMEM((Z, RANK, CUT), BF16),
            pltpu.VMEM((2, PLANE, RANK, CUT), BF16),
            dma((8,)),
            dma,
            dma,
            dma((UP + DOWN,)),
            dma((Z,)),
            dma((Z, Y - 1)),
            dma((Z, Y)),
            dma((Y - 1,)),
            dma((Y,)),
            dma((UP + DOWN, Y)),
            dma((Z, Y)),
            dma((Z,)),
            dma((Z,)),
            dma((X - 1,)),
            dma((X,)),
            dma((X - 1,)),
            dma((X,)),
            dma,
            dma,
            dma((PLANE - 1,)),
            dma((PLANE,)),
            dma((Z - 1,)),
            dma((Z,)),
            dma((PLANE - 1,)),
            dma((PLANE,)),
            dma((PLANE,)),
            dma((PLANE,)),
            dma((2,)),
        ],
        compiler_params=pltpu.CompilerParams(
            collective_id=0, has_side_effects=True, vmem_limit_bytes=64_800_000
        ),
    )(
        gelu_pooled_inner,
        frozen_pooled_trunk_result,
        narrowing_weight.T,
        widening_weight,
        closing_standardize_multiplier.reshape(1, DEPTH),
        closing_standardize_addend.reshape(1, DEPTH),
        closing_projection_weight,
        sentence_encodings,
        logged_sharpening,
        sigmoid_threshold_term,
    )
    pieces = final.reshape(2 * PLANE, RANK, CUT).transpose(1, 0, 2).reshape(RANK, -1).astype(F32)
    return derivative, pieces[:, :INNER].T, pieces[:, INNER : INNER + DEPTH]


def solution(mesh):
    rows = P(("group", "dp"), None)
    return jax.shard_map(
        body,
        mesh=mesh,
        in_specs=(rows, rows, P(), P(), P(), P(), P(), rows, P(), P()),
        out_specs=(rows, P(), P()),
        check_vma=False,
    )
```

```python
import jax
import jax.numpy as jnp
from jax import lax
from jax.experimental import pallas as pl
from jax.experimental.pallas import tpu as pltpu
from jax.sharding import PartitionSpec as P

norm_eps = 1e-06
MESH = pl.DeviceIdType.MESH
BF16, F32 = jnp.bfloat16, jnp.float32

X, YL, YH, Z = 4, 2, 2, 8
Y = YL * YH
ROWS = 56
E, DEPTH, INNER, RANK = 1024, 3072, 12288, 16
PC = 640
QC = E - PC
FORE = 384
IMAGES = X * ROWS
SIDE = Y * ROWS
TEXTS = 2 * SIDE
PLANE = X * Y
CUT = 256
WIDE = 2 * CUT
UP, DOWN = Z // 2, Z // 2 - 1


def remote(src, dst, send_sem, recv_sem, device):
    return pltpu.make_async_remote_copy(
        src_ref=src,
        dst_ref=dst,
        send_sem=send_sem,
        recv_sem=recv_sem,
        device_id=device,
        device_id_type=MESH,
    )


def nt(a, b):
    return lax.dot_general(a, b, (((1,), (1,)), ((), ())), preferred_element_type=F32)


def nn(a, b):
    return lax.dot_general(a, b, (((1,), (0,)), ((), ())), preferred_element_type=F32)


def kernel(
    inner_h,
    trunk_h,
    narrow_h,
    widen_h,
    gain_h,
    bias_h,
    head_h,
    text_h,
    sharp_h,
    shift_h,
    dv_h,
    grad_h,
    inner,
    trunk,
    narrow,
    widen,
    gain,
    bias,
    head,
    text,
    sharp_s,
    shift_s,
    tp,
    tq,
    tile,
    image_wire,
    images,
    dv,
    dv_send,
    dv_recv,
    dv_own,
    unit,
    normed,
    grads,
    pair_send,
    pair_recv,
    plane_send,
    plane_recv,
    ring_recv,
    final,
    load_sem,
    pz_send,
    pz_recv,
    py_send,
    py_recv,
    pf_send,
    pf_recv,
    qy_send,
    qy_recv,
    qz_send,
    qz_recv,
    sp_send,
    sp_recv,
    sq_send,
    sq_recv,
    img_send,
    img_recv,
    rs_send,
    rs_recv,
    pair_ssem,
    pair_rsem,
    plane_ssem,
    plane_rsem,
    ring_ssem,
    ring_rsem,
    back_ssem,
    back_rsem,
    last_ssem,
    last_rsem,
    out_sem,
):
    g, d = lax.axis_index("group"), lax.axis_index("dp")
    c, yh = lax.rem(g, 2), lax.div(g, 2)
    z, yl, x = lax.div(d, YL * X), lax.rem(lax.div(d, X), YL), lax.rem(d, X)
    y = yh * YL + yl
    k = y * X + x

    def device(xx, yy, zz, cc):
        return (
            lax.div(yy, YL) * 2 + cc,
            zz * (YL * X) + lax.rem(yy, YL) * X + xx,
        )

    sibling = device(x, y, z, 1 - c)
    above = device(x, y, lax.rem(z + 1, Z), c)
    below = device(x, y, lax.rem(z + Z - 1, Z), c)

    def at_y(o):
        return lax.rem(y + o, Y)

    def at_x(o):
        return lax.rem(x + o, X)

    def at_z(o):
        return lax.rem(z + o + Z, Z)

    def at_k(o):
        return lax.rem(k + o, PLANE)

    def plane_device(kk):
        return device(lax.rem(kk, X), lax.div(kk, X), z, c)

    loads = [
        pltpu.make_async_copy(text_h, text, load_sem.at[0]),
        pltpu.make_async_copy(inner_h, inner, load_sem.at[1]),
        pltpu.make_async_copy(narrow_h, narrow, load_sem.at[2]),
        pltpu.make_async_copy(widen_h, widen, load_sem.at[3]),
        pltpu.make_async_copy(trunk_h, trunk, load_sem.at[4]),
        pltpu.make_async_copy(gain_h, gain, load_sem.at[5]),
        pltpu.make_async_copy(bias_h, bias, load_sem.at[6]),
        pltpu.make_async_copy(head_h, head, load_sem.at[7]),
        pltpu.make_async_copy(sharp_h, sharp_s, load_sem.at[8]),
        pltpu.make_async_copy(shift_h, shift_s, load_sem.at[9]),
    ]
    barrier = pltpu.get_barrier_semaphore()
    pl.semaphore_signal(barrier, inc=1, device_id=sibling, device_id_type=MESH)

    for neighbour in (above, below):
        pl.semaphore_signal(barrier, inc=1, device_id=neighbour, device_id_type=MESH)
    for o in range(1, Y):
        pl.semaphore_signal(
            barrier, inc=1, device_id=device(x, at_y(o), z, c), device_id_type=MESH
        )
    for o in range(1, X):
        pl.semaphore_signal(
            barrier, inc=1, device_id=device(at_x(o), y, z, c), device_id_type=MESH
        )

    for load in loads:
        load.start()
    pl.semaphore_wait(barrier, 1 + 2 + (Y - 1) + (X - 1))

    pending = []

    loads[0].wait()
    rows = text[...].astype(F32)
    rows = rows * lax.rsqrt(jnp.sum(rows * rows, axis=1, keepdims=True) + norm_eps)
    tp[c, z, y] = rows[:, :PC].astype(BF16)
    tq[c, z, y] = rows[:, PC:].astype(BF16)

    def p_up(zz, hop):
        ref = tp.at[c, zz, y]
        return remote(ref, ref, pz_send.at[hop], pz_recv.at[zz], above)

    def p_down(zz, hop):
        ref = tp.at[c, zz, y]
        return remote(ref, ref, pz_send.at[UP + hop], pz_recv.at[zz], below)

    def p_y(zz, i):
        ref = tp.at[c, zz, y]
        to = device(x, at_y((1, Y - 1)[i]), z, c)
        return remote(ref, ref, py_send.at[zz, i], py_recv.at[zz, i], to)

    def p_y_in(zz, i):
        ref = tp.at[c, zz, at_y((Y - 1, 1)[i])]
        return remote(ref, ref, py_send.at[0, 0], py_recv.at[zz, i], sibling)

    def half_of(ref, i):
        return ref.at[:, pl.ds((0, FORE)[i], (FORE, PC - FORE)[i])]

    def p_far(zz, i):
        ref = half_of(tp.at[c, zz, at_y((Y - 1, 1)[i])], i)
        to = device(x, at_y((1, Y - 1)[i]), z, c)
        return remote(ref, ref, pf_send.at[zz, i], pf_recv.at[zz, i], to)

    def p_far_in(zz, i):
        ref = half_of(tp.at[c, zz, at_y(2)], i)
        return remote(ref, ref, pf_send.at[0, 0], pf_recv.at[zz, i], sibling)

    def q_y(o):
        ref = tq.at[c, z, y]
        return remote(ref, ref, qy_send.at[o - 1], qy_recv.at[y], device(x, at_y(o), z, c))

    def q_y_in(o):
        ref = tq.at[c, z, at_y(o)]
        return remote(ref, ref, qy_send.at[0], qy_recv.at[at_y(o)], sibling)

    def q_up(zz, o, hop):
        ref = tq.at[c, zz, at_y(o)]
        return remote(ref, ref, qz_send.at[hop, o], qz_recv.at[zz, at_y(o)], above)

    def q_down(zz, o, hop):
        ref = tq.at[c, zz, at_y(o)]
        return remote(ref, ref, qz_send.at[UP + hop, o], qz_recv.at[zz, at_y(o)], below)

    def p_across(zz):
        ref = tp.at[c, zz]
        return remote(ref, ref, sp_send.at[zz], sp_recv.at[zz], sibling)

    def q_across(zz):
        ref = tq.at[c, zz]
        return remote(ref, ref, sq_send.at[zz], sq_recv.at[zz], sibling)

    def both(distance):
        if distance == 0:
            return [z]
        return [at_z(-distance), at_z(distance)][: 1 + (distance <= DOWN)]

    p_up(z, 0).start()
    p_down(z, 0).start()
    for i in range(2):
        p_y(z, i).start()
    for o in (1, 3, 2):
        q_y(o).start()
    q_up(z, 0, 0).start()
    q_down(z, 0, 0).start()

    @pending.append
    def _():
        for hop in range(UP):
            p_up(z, hop).wait_send()
        for hop in range(DOWN):
            p_down(z, hop).wait_send()

        @pl.loop(0, Z)
        def _(zz):
            for i in range(2):
                p_y(zz, i).wait_send()
                p_far(zz, i).wait_send()
            p_across(zz).wait_send()
            q_across(zz).wait_send()

        for o in range(1, Y):
            q_y(o).wait_send()

        @pl.loop(0, Y)
        def _(o):
            for hop in range(UP):
                q_up(z, o, hop).wait_send()
            for hop in range(DOWN):
                q_down(z, o, hop).wait_send()

    def p_ring(distance):
        zz = at_z(-distance)
        p_up(zz, 0).wait_recv()
        if distance < UP:
            p_up(zz, distance).start()
        if distance <= DOWN:
            zz = at_z(distance)
            p_down(zz, 0).wait_recv()
            if distance < DOWN:
                p_down(zz, distance).start()
        for zz in both(distance):
            for i in range(2):
                p_y(zz, i).start()

    def p_pass(distance):
        for zz in both(distance):
            for i in range(2):
                p_y_in(zz, i).wait_recv()
                p_far(zz, i).start()

    def p_end(distance):
        for zz in both(distance):
            for i in range(2):
                p_far_in(zz, i).wait_recv()
            p_across(zz).start()

    def q_first():
        for o in (1, 3, 2):
            q_y_in(o).wait_recv()
            q_up(z, o, 0).start()
            q_down(z, o, 0).start()

    def q_ring(distance, others):
        for o in others:
            zz = at_z(-distance)
            q_up(zz, o, 0).wait_recv()
            if distance < UP:
                q_up(zz, o, distance).start()
            if distance <= DOWN:
                zz = at_z(distance)
                q_down(zz, o, 0).wait_recv()
                if distance < DOWN:
                    q_down(zz, o, distance).start()

    def q_end(distance):
        for zz in both(distance):
            q_across(zz).start()

    own, rest = (0,), (1, 3, 2)

    loads[1].wait()
    loads[2].wait()
    step = INNER // 4
    low = jnp.zeros((ROWS, RANK), F32)
    for i in range(4):
        cols = pl.ds(i * step, step)
        low = low + nt(inner[:, cols], narrow[:, cols])
    low = low.astype(BF16)

    p_ring(1)
    p_pass(0)
    q_ring(1, own)
    q_first()
    loads[3].wait()
    loads[4].wait()
    loads[5].wait()
    loads[6].wait()
    section = trunk[...].astype(F32) + nn(low, widen[...])
    centred = section - jnp.mean(section, axis=1, keepdims=True)
    inv_std = lax.rsqrt(jnp.mean(centred * centred, axis=1, keepdims=True) + norm_eps)
    spread = centred * inv_std
    normed[...] = spread
    head_in = (spread * gain[...] + bias[...]).astype(BF16)
    p_ring(2)
    p_pass(1)
    q_ring(1, rest)
    q_ring(2, own)
    loads[7].wait()
    embedding = nn(head_in, head[...])
    inv_len = lax.rsqrt(jnp.sum(embedding * embedding, axis=1, keepdims=True) + norm_eps)
    embedding = embedding * inv_len
    unit[...] = embedding

    half = E // 2

    def to_wire(ref, value):
        ref[...] = jnp.concatenate([value[:, :half], value[:, half:]], axis=0).astype(BF16)

    def from_wire(ref):
        value = ref[...].astype(F32)
        return jnp.concatenate([value[:ROWS], value[ROWS:]], axis=1)

    to_wire(image_wire.at[x], embedding)

    def send_images(o):
        ref = image_wire.at[x]
        return remote(ref, ref, img_send.at[o - 1], img_recv.at[x], device(at_x(o), y, z, c))

    @pl.loop(1, X)
    def _(o):
        send_images(o).start()

    @pending.append
    def _():
        @pl.loop(1, X)
        def _(o):
            send_images(o).wait_send()

    p_ring(3)
    p_pass(2)
    q_ring(2, rest)
    q_ring(3, own)
    p_end(0)
    q_end(0)

    @pl.loop(1, X)
    def _(o):
        ref = image_wire.at[at_x(o)]
        remote(ref, ref, img_send.at[0], img_recv.at[at_x(o)], sibling).wait_recv()

    for i in range(0, X, 2):
        two = jnp.concatenate([from_wire(image_wire.at[i]), from_wire(image_wire.at[i + 1])], axis=0)
        images[pl.ds(i * ROWS, 2 * ROWS)] = two.astype(BF16)

    loads[8].wait()
    loads[9].wait()
    sharp = jnp.exp(jnp.full((1, TEXTS), sharp_s[0], F32))
    shift = jnp.full((1, TEXTS), shift_s[0], F32)
    dv[...] = jnp.zeros_like(dv)
    p_ring(4)
    p_pass(3)

    @pl.loop(0, Z)
    def _(s):
        @pl.when(s == 0)
        def _():
            q_ring(3, rest)
            q_ring(4, own)
            p_end(1)
            q_end(1)

        @pl.when(s == 1)
        def _():
            p_pass(4)

        @pl.when(s == 2)
        def _():
            p_end(2)
            q_end(2)

        @pl.when(s == 3)
        def _():
            p_end(3)
            q_end(3)

        @pl.when(s == 5)
        def _():
            q_ring(4, rest)
            p_end(4)
            q_end(4)

        odd = lax.rem(s, 2)
        zz = at_z((1 - odd) * lax.div(s, 2) - odd * lax.div(s + 1, 2))
        for ref, send, recv in ((tp, sp_send, sp_recv), (tq, sq_send, sq_recv)):
            ref = ref.at[1 - c, zz]
            remote(ref, ref, send.at[0], recv.at[zz], sibling).wait_recv()
        for core in range(2):
            part = pl.ds(core * SIDE, SIDE)
            tile[part, :PC] = tp[core, zz].astype(F32).reshape(SIDE, PC).astype(BF16)
            tile[part, PC:] = tq[core, zz].astype(F32).reshape(SIDE, QC).astype(BF16)
        cosine = nt(images[...], tile[...])
        row = lax.broadcasted_iota(jnp.int32, (IMAGES, TEXTS), 0) - x * ROWS
        col = lax.broadcasted_iota(jnp.int32, (IMAGES, TEXTS), 1) - (c * Y + y) * ROWS
        same = (row == col) & (row >= 0) & (row < ROWS) & (s == 0)
        weights = sharp * (jax.nn.sigmoid(sharp * cosine + shift) - jnp.where(same, 1.0, 0.0))
        dv[...] += nn(weights.astype(BF16), tile[...])

    def send_sum(o):
        return remote(
            dv_send.at[o - 1],
            dv_recv.at[x],
            rs_send.at[o - 1],
            rs_recv.at[x],
            device(at_x(o), y, z, c),
        )

    def rows_of(xx):
        return pl.ds(pl.multiple_of(xx * ROWS, 8), ROWS)

    for o in range(1, X):
        to_wire(dv_send.at[o - 1], dv[rows_of(at_x(o))])
        send_sum(o).start()

    @pending.append
    def _():
        @pl.loop(1, X)
        def _(o):
            send_sum(o).wait_send()
    derivative = dv[rows_of(x)]
    for o in range(1, X):
        ref = dv_recv.at[at_x(o)]
        remote(ref, ref, rs_send.at[0], rs_recv.at[at_x(o)], sibling).wait_recv()
        derivative = derivative + from_wire(ref)
    dv_own[...] = derivative
    dv_copy = pltpu.make_async_copy(dv_own, dv_h, out_sem.at[0])
    dv_copy.start()
    pending.append(dv_copy.wait)

    embedding = unit[...]
    along = jnp.sum(embedding * derivative, axis=1, keepdims=True)
    embed_grad = (inv_len * (derivative - embedding * along)).astype(BF16)
    scaled = nt(embed_grad, head[...]) * gain[...]
    spread = normed[...]
    section_grad = inv_std * (
        scaled
        - jnp.mean(scaled, axis=1, keepdims=True)
        - spread * jnp.mean(scaled * spread, axis=1, keepdims=True)
    )
    section_grad = section_grad.astype(BF16)
    back = nt(widen[...], section_grad).astype(BF16)
    up = lax.dot_general(low, section_grad, (((0,), (0,)), ((), ())), preferred_element_type=F32)
    n_down, n_up = INNER // WIDE, DEPTH // WIDE
    for i in range(2 * PLANE):
        if i < n_down:
            value = nn(back, inner[:, pl.ds(i * WIDE, WIDE)])
        elif i < n_down + n_up:
            value = up[:, (i - n_down) * WIDE : (i - n_down + 1) * WIDE]
        else:
            value = jnp.zeros((RANK, WIDE), F32)
        for h in range(2):
            grads[h, i // PLANE, i % PLANE] = value[:, h * CUT : (h + 1) * CUT]

    def pair_copy(h):
        return remote(pair_send.at[h], pair_recv.at[h], pair_ssem.at[h], pair_rsem.at[h], sibling)

    def plane_copy(h, o):
        kk = at_k(o)
        return remote(
            plane_send.at[h, kk],
            plane_recv.at[h, k],
            plane_ssem.at[h, o - 1],
            plane_rsem.at[h, k],
            plane_device(kk),
        )

    def plane_in(h, o):
        ref = plane_recv.at[h, at_k(o)]
        return remote(ref, ref, plane_ssem.at[0, 0], plane_rsem.at[h, at_k(o)], sibling)

    def ring_copy(h, o):
        ref = ring_recv.at[h, z]
        to = device(x, y, at_z(o), c)
        return remote(ref, ref, ring_ssem.at[h, o - 1], ring_rsem.at[h, z], to)

    def ring_in(h, o):
        ref = ring_recv.at[h, at_z(o)]
        return remote(ref, ref, ring_ssem.at[0, 0], ring_rsem.at[h, at_z(o)], sibling)

    def back_copy(h, o):
        ref = final.at[h, c, k]
        return remote(ref, ref, back_ssem.at[h, o - 1], back_rsem.at[h, k], plane_device(at_k(o)))

    def back_in(h, o):
        ref = final.at[h, c, at_k(o)]
        return remote(ref, ref, back_ssem.at[0, 0], back_rsem.at[h, at_k(o)], sibling)

    def last_copy(h, kk):
        ref = final.at[h, c, kk]
        return remote(ref, ref, last_ssem.at[h, kk], last_rsem.at[h, kk], sibling)

    def last_in(h, kk):
        ref = final.at[h, 1 - c, kk]
        return remote(ref, ref, last_ssem.at[0, 0], last_rsem.at[h, kk], sibling)

    def out_copy(h, core):
        return pltpu.make_async_copy(
            final.at[h, core], grad_h.at[h, core], out_sem.at[1 + 2 * h + core]
        )

    for h in range(2):
        pair_send[h] = grads[h, 1 - c].astype(BF16)
        pair_copy(h).start()
    for h in range(2):
        pair_copy(h).wait_recv()
        plane_send[h] = (grads[h, c] + pair_recv[h].astype(F32)).astype(BF16)

        @pl.loop(1, PLANE)
        def _(o):
            plane_copy(h, o).start()

        plane_recv[h, k] = plane_send[h, k]
    for h in range(2):

        @pl.loop(1, PLANE)
        def _(o):
            plane_in(h, o).wait_recv()

        ring_recv[h, z] = jnp.sum(plane_recv[h].astype(F32), axis=0).astype(BF16)

        @pl.loop(1, Z)
        def _(o):
            ring_copy(h, o).start()

    for h in range(2):

        @pl.loop(1, Z)
        def _(o):
            ring_in(h, o).wait_recv()

        final[h, c, k] = jnp.sum(ring_recv[h].astype(F32), axis=0).astype(BF16)

        @pl.loop(1, PLANE)
        def _(o):
            back_copy(h, o).start()

        last_copy(h, k).start()
    for h in range(2):

        @pl.loop(1, PLANE)
        def _(o):
            back_in(h, o).wait_recv()
            last_copy(h, at_k(o)).start()

        out_copy(h, c).start()
    for h in range(2):

        @pl.loop(0, PLANE)
        def _(kk):
            last_in(h, kk).wait_recv()

        out_copy(h, 1 - c).start()

    @pending.append
    def _():
        for h in range(2):
            pair_copy(h).wait_send()

            @pl.loop(1, PLANE)
            def _(o):
                plane_copy(h, o).wait_send()
                back_copy(h, o).wait_send()

            @pl.loop(1, Z)
            def _(o):
                ring_copy(h, o).wait_send()

            @pl.loop(0, PLANE)
            def _(kk):
                last_copy(h, kk).wait_send()

            for core in range(2):
                out_copy(h, core).wait()

    for wait in pending:
        wait()


def finish(
    dv_h, grad_h, dv_out, down_out, up_out, dv, pieces, whole, in_sem, dv_sem, down_sem, up_sem
):
    reads = [
        pltpu.make_async_copy(dv_h, dv, in_sem.at[0]),
        pltpu.make_async_copy(grad_h, pieces, in_sem.at[1]),
    ]
    for read in reads:
        read.start()
    for read in reads:
        read.wait()
    dv_copy = pltpu.make_async_copy(dv, dv_out, dv_sem)
    dv_copy.start()

    def out(i):
        if i < INNER // DEPTH:
            cols = pl.ds(i * DEPTH, DEPTH)
            return pltpu.make_async_copy(whole.at[:, cols], down_out.at[:, cols], down_sem.at[i])
        return pltpu.make_async_copy(whole.at[:, pl.ds(INNER, DEPTH)], up_out, up_sem)

    count = (INNER + DEPTH) // DEPTH
    for i in range(count):
        for j in range(i * DEPTH // CUT, (i + 1) * DEPTH // CUT):
            piece = pieces[j % 2, j // 2 // PLANE, j // 2 % PLANE]
            whole[:, pl.ds(j * CUT, CUT)] = piece.astype(F32)
        out(i).start()
    for i in range(count):
        out(i).wait()
    dv_copy.wait()


def body(
    gelu_pooled_inner,
    frozen_pooled_trunk_result,
    narrowing_weight,
    widening_weight,
    closing_standardize_multiplier,
    closing_standardize_addend,
    closing_projection_weight,
    sentence_encodings,
    logged_sharpening,
    sigmoid_threshold_term,
):
    anywhere = pl.BlockSpec(memory_space=pl.ANY)
    dma = pltpu.SemaphoreType.DMA
    derivative, pieces = pl.pallas_call(
        kernel,
        out_shape=(
            jax.ShapeDtypeStruct((ROWS, E), F32),
            jax.ShapeDtypeStruct((2, 2, PLANE, RANK, CUT), BF16),
        ),
        in_specs=[anywhere] * 8 + [pl.BlockSpec(memory_space=pltpu.HBM)] * 2,
        out_specs=(anywhere, anywhere),
        scratch_shapes=[
            pltpu.VMEM((ROWS, INNER), BF16),
            pltpu.VMEM((ROWS, DEPTH), BF16),
            pltpu.VMEM((RANK, INNER), BF16),
            pltpu.VMEM((RANK, DEPTH), BF16),
            pltpu.VMEM((1, DEPTH), F32),
            pltpu.VMEM((1, DEPTH), F32),
            pltpu.VMEM((DEPTH, E), BF16),
            pltpu.VMEM((ROWS, E), BF16),
            pltpu.SMEM((1,), F32),
            pltpu.SMEM((1,), F32),
            pltpu.VMEM((2, Z, Y, ROWS, PC), BF16),
            pltpu.VMEM((2, Z, Y, ROWS, QC), BF16),
            pltpu.VMEM((TEXTS, E), BF16),
            pltpu.VMEM((X, 2 * ROWS, E // 2), BF16),
            pltpu.VMEM((IMAGES, E), BF16),
            pltpu.VMEM((IMAGES, E), F32),
            pltpu.VMEM((X - 1, 2 * ROWS, E // 2), BF16),
            pltpu.VMEM((X, 2 * ROWS, E // 2), BF16),
            pltpu.VMEM((ROWS, E), F32),
            pltpu.VMEM((ROWS, E), F32),
            pltpu.VMEM((ROWS, DEPTH), F32),
            pltpu.VMEM((2, 2, PLANE, RANK, CUT), F32),
            pltpu.VMEM((2, PLANE, RANK, CUT), BF16),
            pltpu.VMEM((2, PLANE, RANK, CUT), BF16),
            pltpu.VMEM((2, PLANE, RANK, CUT), BF16),
            pltpu.VMEM((2, PLANE, RANK, CUT), BF16),
            pltpu.VMEM((2, Z, RANK, CUT), BF16),
            pltpu.VMEM((2, 2, PLANE, RANK, CUT), BF16),
            dma((10,)),
            dma((UP + DOWN,)),
            dma((Z,)),
            dma((Z, 2)),
            dma((Z, 2)),
            dma((Z, 2)),
            dma((Z, 2)),
            dma((Y - 1,)),
            dma((Y,)),
            dma((UP + DOWN, Y)),
            dma((Z, Y)),
            dma((Z,)),
            dma((Z,)),
            dma((Z,)),
            dma((Z,)),
            dma((X - 1,)),
            dma((X,)),
            dma((X - 1,)),
            dma((X,)),
            dma((2,)),
            dma((2,)),
            dma((2, PLANE - 1)),
            dma((2, PLANE)),
            dma((2, Z - 1)),
            dma((2, Z)),
            dma((2, PLANE - 1)),
            dma((2, PLANE)),
            dma((2, PLANE)),
            dma((2, PLANE)),
            dma((5,)),
        ],
        compiler_params=pltpu.CompilerParams(
            collective_id=0, has_side_effects=True, vmem_limit_bytes=64_800_000
        ),
    )(
        gelu_pooled_inner,
        frozen_pooled_trunk_result,
        narrowing_weight.T,
        widening_weight,
        closing_standardize_multiplier.reshape(1, DEPTH),
        closing_standardize_addend.reshape(1, DEPTH),
        closing_projection_weight,
        sentence_encodings,
        logged_sharpening,
        sigmoid_threshold_term,
    )
    derivative, down, up = pl.pallas_call(
        finish,
        out_shape=(
            jax.ShapeDtypeStruct((ROWS, E), F32),
            jax.ShapeDtypeStruct((RANK, INNER), F32),
            jax.ShapeDtypeStruct((RANK, DEPTH), F32),
        ),
        in_specs=[anywhere] * 2,
        out_specs=(anywhere,) * 3,
        scratch_shapes=[
            pltpu.VMEM((ROWS, E), F32),
            pltpu.VMEM((2, 2, PLANE, RANK, CUT), BF16),
            pltpu.VMEM((RANK, INNER + DEPTH), F32),
            dma((2,)),
            dma,
            dma((INNER // DEPTH,)),
            dma,
        ],
        compiler_params=pltpu.CompilerParams(vmem_limit_bytes=64_800_000),
    )(derivative, pieces)
    return derivative, down.T, up


def solution(mesh):
    rows = P(("group", "dp"), None)
    return jax.shard_map(
        body,
        mesh=mesh,
        in_specs=(rows, rows, P(), P(), P(), P(), P(), rows, P(), P()),
        out_specs=(rows, P(), P()),
        check_vma=False,
    )
```

```python
import jax
import jax.numpy as jnp
from jax import lax
from jax.experimental import pallas as pl
from jax.experimental.pallas import tpu as pltpu
from jax.sharding import PartitionSpec as P

norm_eps = 1e-06
MESH = pl.DeviceIdType.MESH
BF16, F32 = jnp.bfloat16, jnp.float32

X, YL, YH, Z = 4, 2, 2, 8
Y = YL * YH
ROWS = 56
E, DEPTH, INNER, RANK = 1024, 3072, 12288, 16
PC = 640
QC = E - PC
FORE = 256
SIDE = X * ROWS
IMAGES = 2 * SIDE
TEXTS = Y * ROWS
PLANE = X * Y
CUT = 256
WIDE = 2 * CUT
HOPS = Z // 2 - 1


def remote(src, dst, send_sem, recv_sem, device):
    return pltpu.make_async_remote_copy(
        src_ref=src,
        dst_ref=dst,
        send_sem=send_sem,
        recv_sem=recv_sem,
        device_id=device,
        device_id_type=MESH,
    )


def nt(a, b):
    return lax.dot_general(a, b, (((1,), (1,)), ((), ())), preferred_element_type=F32)


def nn(a, b):
    return lax.dot_general(a, b, (((1,), (0,)), ((), ())), preferred_element_type=F32)


def kernel(
    inner_h,
    trunk_h,
    narrow_h,
    widen_h,
    gain_h,
    bias_h,
    head_h,
    text_h,
    sharp_h,
    shift_h,
    dv_h,
    grad_h,
    inner,
    trunk,
    narrow,
    widen,
    gain,
    bias,
    head,
    text,
    sharp_s,
    shift_s,
    tp,
    tq,
    tile,
    image_wire,
    images,
    dv,
    cross_send,
    cross_recv,
    dv_send,
    dv_recv,
    dv_own,
    unit,
    normed,
    section,
    grads,
    pair_send,
    pair_recv,
    plane_send,
    plane_recv,
    ring_recv,
    final,
    load_sem,
    pz_send,
    pz_recv,
    pt_send,
    pt_recv,
    py_send,
    py_recv,
    pf_send,
    pf_recv,
    qy_send,
    qy_recv,
    qz_send,
    qz_recv,
    img_send,
    img_recv,
    over_send,
    over_recv,
    cross_ssem,
    cross_rsem,
    rs_send,
    rs_recv,
    pair_ssem,
    pair_rsem,
    plane_ssem,
    plane_rsem,
    ring_ssem,
    ring_rsem,
    back_ssem,
    back_rsem,
    last_ssem,
    last_rsem,
    out_sem,
):
    g, d = lax.axis_index("group"), lax.axis_index("dp")
    c, yh = lax.rem(g, 2), lax.div(g, 2)
    z, yl, x = lax.div(d, YL * X), lax.rem(lax.div(d, X), YL), lax.rem(d, X)
    y = yh * YL + yl
    k = y * X + x

    def device(xx, yy, zz, cc):
        return (
            lax.div(yy, YL) * 2 + cc,
            zz * (YL * X) + lax.rem(yy, YL) * X + xx,
        )

    sibling = device(x, y, z, 1 - c)
    above = device(x, y, lax.rem(z + 1, Z), c)
    below = device(x, y, lax.rem(z + Z - 1, Z), c)

    def at_y(o):
        return lax.rem(y + o, Y)

    def at_x(o):
        return lax.rem(x + o, X)

    def at_z(o):
        return lax.rem(z + o + Z, Z)

    def at_k(o):
        return lax.rem(k + o, PLANE)

    def plane_device(kk):
        return device(lax.rem(kk, X), lax.div(kk, X), z, c)

    loads = [
        pltpu.make_async_copy(text_h, text, load_sem.at[0]),
        pltpu.make_async_copy(inner_h, inner, load_sem.at[1]),
        pltpu.make_async_copy(narrow_h, narrow, load_sem.at[2]),
        pltpu.make_async_copy(widen_h, widen, load_sem.at[3]),
        pltpu.make_async_copy(trunk_h, trunk, load_sem.at[4]),
        pltpu.make_async_copy(gain_h, gain, load_sem.at[5]),
        pltpu.make_async_copy(bias_h, bias, load_sem.at[6]),
        pltpu.make_async_copy(head_h, head, load_sem.at[7]),
        pltpu.make_async_copy(sharp_h, sharp_s, load_sem.at[8]),
        pltpu.make_async_copy(shift_h, shift_s, load_sem.at[9]),
    ]
    loads[0].start()
    barrier = pltpu.get_barrier_semaphore()
    pl.semaphore_signal(barrier, inc=1, device_id=sibling, device_id_type=MESH)

    for neighbour in (above, below):
        pl.semaphore_signal(barrier, inc=1, device_id=neighbour, device_id_type=MESH)
    for o in range(1, Y):
        pl.semaphore_signal(
            barrier, inc=1, device_id=device(x, at_y(o), z, c), device_id_type=MESH
        )
    for o in range(1, X):
        pl.semaphore_signal(
            barrier, inc=1, device_id=device(at_x(o), y, z, c), device_id_type=MESH
        )

    for load in loads[1:]:
        load.start()
    pending = []

    loads[0].wait()
    rows = text[...].astype(F32)
    rows = rows * lax.rsqrt(jnp.sum(rows * rows, axis=1, keepdims=True) + norm_eps)
    tp[c, z, y] = rows[:, :PC].astype(BF16)
    tq[c, z, y] = rows[:, PC:].astype(BF16)

    pl.semaphore_wait(barrier, 1 + 2 + (Y - 1) + (X - 1))

    def p_up(zz, hop):
        ref = tp.at[c, zz, y]
        return remote(ref, ref, pz_send.at[hop], pz_recv.at[zz], above)

    def p_down(zz, hop):
        ref = tp.at[c, zz, y]
        return remote(ref, ref, pz_send.at[HOPS + hop], pz_recv.at[zz], below)

    def half_of(ref, i):
        return ref.at[:, pl.ds((0, FORE)[i], (FORE, PC - FORE)[i])]

    def p_turn(zz, i):
        ref = half_of(tp.at[c, zz, y], i)
        return remote(ref, ref, pt_send.at[i], pt_recv.at[i], (above, below)[i])

    def p_y(zz, i):
        ref = tp.at[c, zz, y]
        to = device(x, at_y((1, Y - 1, 2)[i]), z, c)
        return remote(ref, ref, py_send.at[zz, i], py_recv.at[zz, i], to)

    def p_y_in(zz, i):
        ref = tp.at[c, zz, at_y((Y - 1, 1, 2)[i])]
        return remote(ref, ref, py_send.at[0, 0], py_recv.at[zz, i], sibling)

    def p_far(zz, i):
        ref = half_of(tp.at[c, zz, at_y((Y - 1, 1)[i])], i)
        to = device(x, at_y((1, Y - 1)[i]), z, c)
        return remote(ref, ref, pf_send.at[zz, i], pf_recv.at[zz, i], to)

    def p_far_in(zz, i):
        ref = half_of(tp.at[c, zz, at_y(2)], i)
        return remote(ref, ref, pf_send.at[0, 0], pf_recv.at[zz, i], sibling)

    def q_y(o):
        ref = tq.at[c, z, y]
        return remote(ref, ref, qy_send.at[o - 1], qy_recv.at[y], device(x, at_y(o), z, c))

    def q_y_in(o):
        ref = tq.at[c, z, at_y(o)]
        return remote(ref, ref, qy_send.at[0], qy_recv.at[at_y(o)], sibling)

    def q_up(zz, o, hop):
        ref = tq.at[c, zz, at_y(o)]
        return remote(ref, ref, qz_send.at[hop, o], qz_recv.at[zz, at_y(o)], above)

    def q_down(zz, o, hop):
        ref = tq.at[c, zz, at_y(o)]
        return remote(ref, ref, qz_send.at[HOPS + 1 + hop, o], qz_recv.at[zz, at_y(o)], below)

    def both(distance):
        if distance in (0, Z // 2):
            return [at_z(distance)]
        return [at_z(-distance), at_z(distance)]

    def p_spread(zz, whole):
        for i in range(2 + whole):
            p_y(zz, i).start()

    p_up(z, 0).start()
    p_down(z, 0).start()
    p_spread(z, False)
    for o in (1, 3, 2):
        q_y(o).start()
    q_up(z, 0, 0).start()
    q_down(z, 0, 0).start()

    def last_hop(o):
        return (q_up, q_down)[o % 2]

    @pending.append
    def _():
        for hop in range(HOPS):
            p_up(z, hop).wait_send()
            p_down(z, hop).wait_send()
        for i in range(2):
            p_turn(z, i).wait_send()

        @pl.loop(0, Z)
        def _(zz):
            for i in range(2):
                p_y(zz, i).wait_send()

        @pl.loop(0, Z - 1)
        def _(zz):
            for i in range(2):
                p_far(at_z(zz + Z // 2 + 1), i).wait_send()

        p_y(at_z(Z // 2), 2).wait_send()
        for o in range(1, Y):
            q_y(o).wait_send()
        for o in range(Y):
            for hop in range(HOPS):
                q_up(z, o, hop).wait_send()
                q_down(z, o, hop).wait_send()
            last_hop(o)(z, o, HOPS).wait_send()

    def p_ring(distance):
        if distance > HOPS:
            zz = at_z(distance)
            for i in range(2):
                p_turn(zz, i).wait_recv()
            p_spread(zz, True)
            return
        for i, (send, zz) in enumerate(((p_up, at_z(-distance)), (p_down, at_z(distance)))):
            send(zz, 0).wait_recv()
            if distance < HOPS:
                send(zz, distance).start()
            else:
                p_turn(zz, i).start()
            p_spread(zz, False)

    def p_pass(distance):
        for zz in both(distance):
            for i in range(2):
                p_y_in(zz, i).wait_recv()
                if distance <= HOPS:
                    p_far(zz, i).start()

    def p_end(distance):
        for zz in both(distance):
            if distance <= HOPS:
                for i in range(2):
                    p_far_in(zz, i).wait_recv()
            else:
                p_y_in(zz, 2).wait_recv()

    def q_first():
        for o in (1, 3, 2):
            q_y_in(o).wait_recv()
            q_up(z, o, 0).start()
            q_down(z, o, 0).start()

    def q_ring(distance, others):
        for o in others:
            for send, zz in ((q_up, at_z(-distance)), (q_down, at_z(distance))):
                if distance <= HOPS or send is last_hop(o):
                    send(zz, o, 0).wait_recv()
                if distance < HOPS or (distance == HOPS and send is last_hop(o)):
                    send(zz, o, distance).start()

    own, rest = (0,), (1, 3, 2)

    loads[1].wait()
    loads[2].wait()
    step = INNER // 4
    low = jnp.zeros((ROWS, RANK), F32)
    for i in range(4):
        cols = pl.ds(i * step, step)
        low = low + nt(inner[:, cols], narrow[:, cols])
    low = low.astype(BF16)

    loads[3].wait()
    loads[4].wait()
    loads[5].wait()
    loads[6].wait()
    trailing = trunk[...].astype(F32) + nn(low, widen[...])
    centred = trailing - jnp.mean(trailing, axis=1, keepdims=True)
    inv_std = lax.rsqrt(jnp.mean(centred * centred, axis=1, keepdims=True) + norm_eps)
    spread = centred * inv_std
    normed[...] = spread
    head_in = (spread * gain[...] + bias[...]).astype(BF16)
    p_ring(1)
    p_pass(0)
    q_ring(1, own)
    q_first()
    loads[7].wait()
    embedding = nn(head_in, head[...])
    inv_len = lax.rsqrt(jnp.sum(embedding * embedding, axis=1, keepdims=True) + norm_eps)
    embedding = embedding * inv_len
    unit[...] = embedding

    half = E // 2

    def to_wire(ref, value):
        ref[...] = jnp.concatenate([value[:, :half], value[:, half:]], axis=0).astype(BF16)

    def from_wire(ref):
        value = ref[...].astype(F32)
        return jnp.concatenate([value[:ROWS], value[ROWS:]], axis=1)

    to_wire(image_wire.at[c, x], embedding)

    def send_images(o):
        ref = image_wire.at[c, x]
        return remote(ref, ref, img_send.at[o - 1], img_recv.at[x], device(at_x(o), y, z, c))

    def images_over(xx):
        ref = image_wire.at[c, xx]
        return remote(ref, ref, over_send.at[xx], over_recv.at[xx], sibling)

    @pl.loop(1, X)
    def _(o):
        send_images(o).start()

    images_over(x).start()

    @pending.append
    def _():
        @pl.loop(1, X)
        def _(o):
            send_images(o).wait_send()

        @pl.loop(0, X)
        def _(xx):
            images_over(xx).wait_send()

    p_ring(2)
    p_pass(1)
    q_ring(1, rest)
    q_ring(2, own)
    p_ring(3)
    p_pass(2)
    q_ring(2, rest)
    q_ring(3, own)
    p_end(0)

    @pl.loop(1, X)
    def _(o):
        ref = image_wire.at[c, at_x(o)]
        remote(ref, ref, img_send.at[0], img_recv.at[at_x(o)], sibling).wait_recv()
        images_over(at_x(o)).start()

    @pl.loop(0, X)
    def _(xx):
        ref = image_wire.at[1 - c, xx]
        remote(ref, ref, over_send.at[0], over_recv.at[xx], sibling).wait_recv()

    for i in range(0, 2 * X, 2):
        two = [from_wire(image_wire.at[j // X, j % X]) for j in (i, i + 1)]
        images[pl.ds(i * ROWS, 2 * ROWS)] = jnp.concatenate(two, axis=0).astype(BF16)

    loads[8].wait()
    loads[9].wait()
    sharp = jnp.exp(jnp.full((1, 2 * TEXTS), sharp_s[0], F32))
    shift = jnp.full((1, 2 * TEXTS), shift_s[0], F32)
    dv[...] = jnp.zeros_like(dv)

    @pl.loop(0, Z // 2 + 1)
    def _(s):
        @pl.when(s == 1)
        def _():
            p_ring(4)
            p_pass(3)
            p_end(1)

        @pl.when(s == 2)
        def _():
            q_ring(3, rest)
            p_end(2)

        @pl.when(s == 3)
        def _():
            p_end(3)

        @pl.when(s == 4)
        def _():
            q_ring(4, own + rest)
            p_pass(4)
            p_end(4)

        def fill(i, zz):
            part = pl.ds(i * TEXTS, TEXTS)
            tile[part, :PC] = tp[c, zz].astype(F32).reshape(TEXTS, PC).astype(BF16)
            tile[part, PC:] = tq[c, zz].astype(F32).reshape(TEXTS, QC).astype(BF16)

        fill(0, at_z(-s))
        single = (s == 0) | (s == Z // 2)

        @pl.when(single)
        def _():
            tile[pl.ds(TEXTS, TEXTS)] = jnp.zeros((TEXTS, E), BF16)

        @pl.when(jnp.logical_not(single))
        def _():
            fill(1, at_z(s))

        cosine = nt(images[...], tile[...])
        row = lax.broadcasted_iota(jnp.int32, cosine.shape, 0) - (c * X + x) * ROWS
        col = lax.broadcasted_iota(jnp.int32, cosine.shape, 1) - y * ROWS
        same = (row == col) & (row >= 0) & (row < ROWS) & (s == 0)
        weights = sharp * (jax.nn.sigmoid(sharp * cosine + shift) - jnp.where(same, 1.0, 0.0))
        dv[...] += nn(weights.astype(BF16), tile[...])

    def send_sum(o):
        return remote(
            dv_send.at[o - 1],
            dv_recv.at[x],
            rs_send.at[o - 1],
            rs_recv.at[x],
            device(at_x(o), y, z, c),
        )

    def cross(o):
        return remote(
            cross_send.at[o], cross_recv.at[o], cross_ssem.at[o], cross_rsem.at[o], sibling
        )

    def rows_of(core, xx):
        return pl.ds(pl.multiple_of((core * X + xx) * ROWS, 8), ROWS)

    order = (*range(1, X), 0)
    for o in order:
        to_wire(cross_send.at[o], dv[rows_of(1 - c, at_x(o))])
        cross(o).start()
    for o in order:
        cross(o).wait_recv()
        derivative = dv[rows_of(c, at_x(o))] + from_wire(cross_recv.at[o])
        if o > 0:
            to_wire(dv_send.at[o - 1], derivative)
            send_sum(o).start()

    @pending.append
    def _():
        for o in range(X):
            cross(o).wait_send()
            if o > 0:
                send_sum(o).wait_send()

    for o in range(1, X):
        ref = dv_recv.at[at_x(o)]
        remote(ref, ref, rs_send.at[0], rs_recv.at[at_x(o)], sibling).wait_recv()
        derivative = derivative + from_wire(ref)
    dv_own[...] = derivative
    dv_copy = pltpu.make_async_copy(dv_own, dv_h, out_sem.at[0])
    dv_copy.start()
    pending.append(dv_copy.wait)

    embedding = unit[...]
    along = jnp.sum(embedding * derivative, axis=1, keepdims=True)
    embed_grad = (inv_len * (derivative - embedding * along)).astype(BF16)
    scaled = nt(embed_grad, head[...]) * gain[...]
    spread = normed[...]
    section_grad = inv_std * (
        scaled
        - jnp.mean(scaled, axis=1, keepdims=True)
        - spread * jnp.mean(scaled * spread, axis=1, keepdims=True)
    )
    section_grad = section_grad.astype(BF16)
    section[...] = section_grad
    back = nt(widen[...], section_grad).astype(BF16)

    n_down, n_up = INNER // WIDE // 2, DEPTH // WIDE // 2

    def piece(i, core):
        if i < n_down:
            cols = pl.ds(pl.multiple_of((2 * i + core) * WIDE, WIDE), WIDE)
            return nn(back, inner[:, cols])
        if i < n_down + n_up:
            cols = pl.ds(pl.multiple_of((2 * (i - n_down) + core) * WIDE, WIDE), WIDE)
            dims = (((0,), (0,)), ((), ()))
            return lax.dot_general(low, section[:, cols], dims, preferred_element_type=F32)
        return jnp.zeros((RANK, WIDE), F32)

    def pair_copy(h):
        return remote(pair_send.at[h], pair_recv.at[h], pair_ssem.at[h], pair_rsem.at[h], sibling)

    def plane_copy(h, o):
        kk = at_k(o)
        return remote(
            plane_send.at[h, kk],
            plane_recv.at[h, k],
            plane_ssem.at[h, o - 1],
            plane_rsem.at[h, k],
            plane_device(kk),
        )

    def plane_in(h, o):
        ref = plane_recv.at[h, at_k(o)]
        return remote(ref, ref, plane_ssem.at[0, 0], plane_rsem.at[h, at_k(o)], sibling)

    def ring_copy(h, o):
        ref = ring_recv.at[h, z]
        to = device(x, y, at_z(o), c)
        return remote(ref, ref, ring_ssem.at[h, o - 1], ring_rsem.at[h, z], to)

    def ring_in(h, o):
        ref = ring_recv.at[h, at_z(o)]
        return remote(ref, ref, ring_ssem.at[0, 0], ring_rsem.at[h, at_z(o)], sibling)

    def back_copy(h, o):
        ref = final.at[h, c, k]
        return remote(ref, ref, back_ssem.at[h, o - 1], back_rsem.at[h, k], plane_device(at_k(o)))

    def back_in(h, o):
        ref = final.at[h, c, at_k(o)]
        return remote(ref, ref, back_ssem.at[0, 0], back_rsem.at[h, at_k(o)], sibling)

    def last_copy(h, kk):
        ref = final.at[h, c, kk]
        return remote(ref, ref, last_ssem.at[h, kk], last_rsem.at[h, kk], sibling)

    def last_in(h, kk):
        ref = final.at[h, 1 - c, kk]
        return remote(ref, ref, last_ssem.at[0, 0], last_rsem.at[h, kk], sibling)

    def out_copy(h, core):
        return pltpu.make_async_copy(
            final.at[h, core], grad_h.at[h, core], out_sem.at[1 + 2 * h + core]
        )

    for i in range(PLANE):
        value = piece(i, 1 - c).astype(BF16)
        for h in range(2):
            pair_send[h, i] = value[:, h * CUT : (h + 1) * CUT]
    for h in range(2):
        pair_copy(h).start()
    for i in range(PLANE):
        value = piece(i, c)
        for h in range(2):
            grads[h, i] = value[:, h * CUT : (h + 1) * CUT]
    for h in range(2):
        pair_copy(h).wait_recv()
        plane_send[h] = (grads[h] + pair_recv[h].astype(F32)).astype(BF16)

        @pl.loop(1, PLANE)
        def _(o):
            plane_copy(h, o).start()

        plane_recv[h, k] = plane_send[h, k]
    for h in range(2):

        @pl.loop(1, PLANE)
        def _(o):
            plane_in(h, o).wait_recv()

        ring_recv[h, z] = jnp.sum(plane_recv[h].astype(F32), axis=0).astype(BF16)

        @pl.loop(1, Z)
        def _(o):
            ring_copy(h, o).start()

    for h in range(2):

        @pl.loop(1, Z)
        def _(o):
            ring_in(h, o).wait_recv()

        final[h, c, k] = jnp.sum(ring_recv[h].astype(F32), axis=0).astype(BF16)

        @pl.loop(1, PLANE)
        def _(o):
            back_copy(h, o).start()

        last_copy(h, k).start()
    for h in range(2):

        @pl.loop(1, PLANE)
        def _(o):
            back_in(h, o).wait_recv()
            last_copy(h, at_k(o)).start()

        out_copy(h, c).start()
    for h in range(2):

        @pl.loop(0, PLANE)
        def _(kk):
            last_in(h, kk).wait_recv()

        out_copy(h, 1 - c).start()

    @pending.append
    def _():
        for h in range(2):
            pair_copy(h).wait_send()

            @pl.loop(1, PLANE)
            def _(o):
                plane_copy(h, o).wait_send()
                back_copy(h, o).wait_send()

            @pl.loop(1, Z)
            def _(o):
                ring_copy(h, o).wait_send()

            @pl.loop(0, PLANE)
            def _(kk):
                last_copy(h, kk).wait_send()

            for core in range(2):
                out_copy(h, core).wait()

    for wait in pending:
        wait()


def finish(
    dv_h, grad_h, dv_out, down_out, up_out, dv, pieces, whole, in_sem, dv_sem, down_sem, up_sem
):
    reads = [
        pltpu.make_async_copy(dv_h, dv, in_sem.at[0]),
        pltpu.make_async_copy(grad_h, pieces, in_sem.at[1]),
    ]
    for read in reads:
        read.start()
    for read in reads:
        read.wait()
    dv_copy = pltpu.make_async_copy(dv, dv_out, dv_sem)
    dv_copy.start()

    def out(i):
        if i < INNER // DEPTH:
            cols = pl.ds(i * DEPTH, DEPTH)
            return pltpu.make_async_copy(whole.at[:, cols], down_out.at[:, cols], down_sem.at[i])
        return pltpu.make_async_copy(whole.at[:, pl.ds(INNER, DEPTH)], up_out, up_sem)

    count = (INNER + DEPTH) // DEPTH
    for i in range(count):
        for j in range(i * DEPTH // CUT, (i + 1) * DEPTH // CUT):
            piece = pieces[j % 2, j // 2 % 2, j // 4]
            whole[:, pl.ds(j * CUT, CUT)] = piece.astype(F32)
        out(i).start()
    for i in range(count):
        out(i).wait()
    dv_copy.wait()


def body(
    gelu_pooled_inner,
    frozen_pooled_trunk_result,
    narrowing_weight,
    widening_weight,
    closing_standardize_multiplier,
    closing_standardize_addend,
    closing_projection_weight,
    sentence_encodings,
    logged_sharpening,
    sigmoid_threshold_term,
):
    anywhere = pl.BlockSpec(memory_space=pl.ANY)
    dma = pltpu.SemaphoreType.DMA
    derivative, pieces = pl.pallas_call(
        kernel,
        out_shape=(
            jax.ShapeDtypeStruct((ROWS, E), F32),
            jax.ShapeDtypeStruct((2, 2, PLANE, RANK, CUT), BF16),
        ),
        in_specs=[anywhere] * 8 + [pl.BlockSpec(memory_space=pltpu.HBM)] * 2,
        out_specs=(anywhere, anywhere),
        scratch_shapes=[
            pltpu.VMEM((ROWS, INNER), BF16),
            pltpu.VMEM((ROWS, DEPTH), BF16),
            pltpu.VMEM((RANK, INNER), BF16),
            pltpu.VMEM((RANK, DEPTH), BF16),
            pltpu.VMEM((1, DEPTH), F32),
            pltpu.VMEM((1, DEPTH), F32),
            pltpu.VMEM((DEPTH, E), BF16),
            pltpu.VMEM((ROWS, E), BF16),
            pltpu.SMEM((1,), F32),
            pltpu.SMEM((1,), F32),
            pltpu.VMEM((2, Z, Y, ROWS, PC), BF16),
            pltpu.VMEM((2, Z, Y, ROWS, QC), BF16),
            pltpu.VMEM((2 * TEXTS, E), BF16),
            pltpu.VMEM((2, X, 2 * ROWS, E // 2), BF16),
            pltpu.VMEM((IMAGES, E), BF16),
            pltpu.VMEM((IMAGES, E), F32),
            pltpu.VMEM((X, 2 * ROWS, E // 2), BF16),
            pltpu.VMEM((X, 2 * ROWS, E // 2), BF16),
            pltpu.VMEM((X - 1, 2 * ROWS, E // 2), BF16),
            pltpu.VMEM((X, 2 * ROWS, E // 2), BF16),
            pltpu.VMEM((ROWS, E), F32),
            pltpu.VMEM((ROWS, E), F32),
            pltpu.VMEM((ROWS, DEPTH), F32),
            pltpu.VMEM((ROWS, DEPTH), BF16),
            pltpu.VMEM((2, PLANE, RANK, CUT), F32),
            pltpu.VMEM((2, PLANE, RANK, CUT), BF16),
            pltpu.VMEM((2, PLANE, RANK, CUT), BF16),
            pltpu.VMEM((2, PLANE, RANK, CUT), BF16),
            pltpu.VMEM((2, PLANE, RANK, CUT), BF16),
            pltpu.VMEM((2, Z, RANK, CUT), BF16),
            pltpu.VMEM((2, 2, PLANE, RANK, CUT), BF16),
            dma((10,)),
            dma((2 * HOPS,)),
            dma((Z,)),
            dma((2,)),
            dma((2,)),
            dma((Z, 3)),
            dma((Z, 3)),
            dma((Z, 2)),
            dma((Z, 2)),
            dma((Y - 1,)),
            dma((Y,)),
            dma((2 * HOPS + 2, Y)),
            dma((Z, Y)),
            dma((X - 1,)),
            dma((X,)),
            dma((X,)),
            dma((X,)),
            dma((X,)),
            dma((X,)),
            dma((X - 1,)),
            dma((X,)),
            dma((2,)),
            dma((2,)),
            dma((2, PLANE - 1)),
            dma((2, PLANE)),
            dma((2, Z - 1)),
            dma((2, Z)),
            dma((2, PLANE - 1)),
            dma((2, PLANE)),
            dma((2, PLANE)),
            dma((2, PLANE)),
            dma((5,)),
        ],
        compiler_params=pltpu.CompilerParams(
            collective_id=0, has_side_effects=True, vmem_limit_bytes=64_800_000
        ),
    )(
        gelu_pooled_inner,
        frozen_pooled_trunk_result,
        narrowing_weight.T,
        widening_weight,
        closing_standardize_multiplier.reshape(1, DEPTH),
        closing_standardize_addend.reshape(1, DEPTH),
        closing_projection_weight,
        sentence_encodings,
        logged_sharpening,
        sigmoid_threshold_term,
    )
    derivative, down, up = pl.pallas_call(
        finish,
        out_shape=(
            jax.ShapeDtypeStruct((ROWS, E), F32),
            jax.ShapeDtypeStruct((RANK, INNER), F32),
            jax.ShapeDtypeStruct((RANK, DEPTH), F32),
        ),
        in_specs=[anywhere] * 2,
        out_specs=(anywhere,) * 3,
        scratch_shapes=[
            pltpu.VMEM((ROWS, E), F32),
            pltpu.VMEM((2, 2, PLANE, RANK, CUT), BF16),
            pltpu.VMEM((RANK, INNER + DEPTH), F32),
            dma((2,)),
            dma,
            dma((INNER // DEPTH,)),
            dma,
        ],
        compiler_params=pltpu.CompilerParams(vmem_limit_bytes=64_800_000),
    )(derivative, pieces)
    return derivative, down.T, up


def solution(mesh):
    rows = P(("group", "dp"), None)
    return jax.shard_map(
        body,
        mesh=mesh,
        in_specs=(rows, rows, P(), P(), P(), P(), P(), rows, P(), P()),
        out_specs=(rows, P(), P()),
        check_vma=False,
    )
```

```python
import jax
import jax.numpy as jnp
from jax import lax
from jax.experimental import pallas as pl
from jax.experimental.pallas import tpu as pltpu
from jax.sharding import PartitionSpec as P

norm_eps = 1e-06
MESH = pl.DeviceIdType.MESH
BF16, F32 = jnp.bfloat16, jnp.float32

X, YL, YH, Z = 4, 2, 2, 8
Y = YL * YH
ROWS = 56
E, DEPTH, INNER, RANK = 1024, 3072, 12288, 16
PC = 640
QC = E - PC
FORE = 256
SIDE = X * ROWS
IMAGES = 2 * SIDE
TEXTS = Y * ROWS
PLANE = X * Y
WIDE = 512
PARTS = 2
CUT = WIDE // PARTS
HOPS = Z // 2 - 1


def remote(src, dst, send_sem, recv_sem, device):
    return pltpu.make_async_remote_copy(
        src_ref=src,
        dst_ref=dst,
        send_sem=send_sem,
        recv_sem=recv_sem,
        device_id=device,
        device_id_type=MESH,
    )


def nt(a, b):
    return lax.dot_general(a, b, (((1,), (1,)), ((), ())), preferred_element_type=F32)


def nn(a, b):
    return lax.dot_general(a, b, (((1,), (0,)), ((), ())), preferred_element_type=F32)


def kernel(
    inner_h,
    trunk_h,
    narrow_h,
    widen_h,
    gain_h,
    bias_h,
    head_h,
    text_h,
    sharp_h,
    shift_h,
    dv_h,
    grad_h,
    inner,
    trunk,
    narrow,
    widen,
    gain,
    bias,
    head,
    text,
    sharp_s,
    shift_s,
    tp,
    tq,
    tile,
    image_wire,
    images,
    dv,
    cross_send,
    cross_recv,
    dv_send,
    dv_recv,
    dv_own,
    unit,
    normed,
    section,
    grads,
    pair_send,
    pair_recv,
    plane_send,
    plane_recv,
    ring_recv,
    final,
    load_sem,
    pz_send,
    pz_recv,
    pt_send,
    pt_recv,
    py_send,
    py_recv,
    pf_send,
    pf_recv,
    qy_send,
    qy_recv,
    qz_send,
    qz_recv,
    img_send,
    img_recv,
    over_send,
    over_recv,
    cross_ssem,
    cross_rsem,
    rs_send,
    rs_recv,
    pair_ssem,
    pair_rsem,
    plane_ssem,
    plane_rsem,
    ring_ssem,
    ring_rsem,
    back_ssem,
    back_rsem,
    last_ssem,
    last_rsem,
    out_sem,
):
    g, d = lax.axis_index("group"), lax.axis_index("dp")
    c, yh = lax.rem(g, 2), lax.div(g, 2)
    z, yl, x = lax.div(d, YL * X), lax.rem(lax.div(d, X), YL), lax.rem(d, X)
    y = yh * YL + yl
    k = y * X + x

    def device(xx, yy, zz, cc):
        return (
            lax.div(yy, YL) * 2 + cc,
            zz * (YL * X) + lax.rem(yy, YL) * X + xx,
        )

    sibling = device(x, y, z, 1 - c)
    above = device(x, y, lax.rem(z + 1, Z), c)
    below = device(x, y, lax.rem(z + Z - 1, Z), c)

    def at_y(o):
        return lax.rem(y + o, Y)

    def at_x(o):
        return lax.rem(x + o, X)

    def at_z(o):
        return lax.rem(z + o + Z, Z)

    def at_k(o):
        return lax.rem(k + o, PLANE)

    def plane_device(kk):
        return device(lax.rem(kk, X), lax.div(kk, X), z, c)

    loads = [
        pltpu.make_async_copy(text_h, text, load_sem.at[0]),
        pltpu.make_async_copy(inner_h, inner, load_sem.at[1]),
        pltpu.make_async_copy(narrow_h, narrow, load_sem.at[2]),
        pltpu.make_async_copy(widen_h, widen, load_sem.at[3]),
        pltpu.make_async_copy(trunk_h, trunk, load_sem.at[4]),
        pltpu.make_async_copy(gain_h, gain, load_sem.at[5]),
        pltpu.make_async_copy(bias_h, bias, load_sem.at[6]),
        pltpu.make_async_copy(head_h, head, load_sem.at[7]),
        pltpu.make_async_copy(sharp_h, sharp_s, load_sem.at[8]),
        pltpu.make_async_copy(shift_h, shift_s, load_sem.at[9]),
    ]
    loads[0].start()
    barrier = pltpu.get_barrier_semaphore()
    pl.semaphore_signal(barrier, inc=1, device_id=sibling, device_id_type=MESH)

    for neighbour in (above, below):
        pl.semaphore_signal(barrier, inc=1, device_id=neighbour, device_id_type=MESH)
    for o in range(1, Y):
        pl.semaphore_signal(
            barrier, inc=1, device_id=device(x, at_y(o), z, c), device_id_type=MESH
        )
    for o in range(1, X):
        pl.semaphore_signal(
            barrier, inc=1, device_id=device(at_x(o), y, z, c), device_id_type=MESH
        )

    for load in loads[1:]:
        load.start()
    pending = []

    loads[0].wait()
    rows = text[...].astype(F32)
    rows = rows * lax.rsqrt(jnp.sum(rows * rows, axis=1, keepdims=True) + norm_eps)
    tp[c, z, y] = rows[:, :PC].astype(BF16)
    tq[c, z, y] = rows[:, PC:].astype(BF16)

    pl.semaphore_wait(barrier, 1 + 2 + (Y - 1) + (X - 1))

    def p_up(zz, hop):
        ref = tp.at[c, zz, y]
        return remote(ref, ref, pz_send.at[hop], pz_recv.at[zz], above)

    def p_down(zz, hop):
        ref = tp.at[c, zz, y]
        return remote(ref, ref, pz_send.at[HOPS + hop], pz_recv.at[zz], below)

    def half_of(ref, i):
        return ref.at[:, pl.ds((0, FORE)[i], (FORE, PC - FORE)[i])]

    def p_turn(zz, i):
        ref = half_of(tp.at[c, zz, y], i)
        return remote(ref, ref, pt_send.at[i], pt_recv.at[i], (above, below)[i])

    def p_y(zz, i):
        ref = tp.at[c, zz, y]
        to = device(x, at_y((1, Y - 1, 2)[i]), z, c)
        return remote(ref, ref, py_send.at[zz, i], py_recv.at[zz, i], to)

    def p_y_in(zz, i):
        ref = tp.at[c, zz, at_y((Y - 1, 1, 2)[i])]
        return remote(ref, ref, py_send.at[0, 0], py_recv.at[zz, i], sibling)

    def p_far(zz, i):
        ref = half_of(tp.at[c, zz, at_y((Y - 1, 1)[i])], i)
        to = device(x, at_y((1, Y - 1)[i]), z, c)
        return remote(ref, ref, pf_send.at[zz, i], pf_recv.at[zz, i], to)

    def p_far_in(zz, i):
        ref = half_of(tp.at[c, zz, at_y(2)], i)
        return remote(ref, ref, pf_send.at[0, 0], pf_recv.at[zz, i], sibling)

    def q_y(o):
        ref = tq.at[c, z, y]
        return remote(ref, ref, qy_send.at[o - 1], qy_recv.at[y], device(x, at_y(o), z, c))

    def q_y_in(o):
        ref = tq.at[c, z, at_y(o)]
        return remote(ref, ref, qy_send.at[0], qy_recv.at[at_y(o)], sibling)

    def q_up(zz, o, hop):
        ref = tq.at[c, zz, at_y(o)]
        return remote(ref, ref, qz_send.at[hop, o], qz_recv.at[zz, at_y(o)], above)

    def q_down(zz, o, hop):
        ref = tq.at[c, zz, at_y(o)]
        return remote(ref, ref, qz_send.at[HOPS + 1 + hop, o], qz_recv.at[zz, at_y(o)], below)

    def both(distance):
        if distance in (0, Z // 2):
            return [at_z(distance)]
        return [at_z(-distance), at_z(distance)]

    def p_spread(zz, whole):
        for i in range(2 + whole):
            p_y(zz, i).start()

    p_up(z, 0).start()
    p_down(z, 0).start()
    p_spread(z, False)
    for o in (2, 1, 3):
        q_y(o).start()
    q_up(z, 0, 0).start()
    q_down(z, 0, 0).start()

    def last_hop(o):
        return (q_up, q_down)[o % 2]

    @pending.append
    def _():
        for hop in range(HOPS):
            p_up(z, hop).wait_send()
            p_down(z, hop).wait_send()
        for i in range(2):
            p_turn(z, i).wait_send()

        @pl.loop(0, Z)
        def _(zz):
            for i in range(2):
                p_y(zz, i).wait_send()

        @pl.loop(0, Z - 1)
        def _(zz):
            for i in range(2):
                p_far(at_z(zz + Z // 2 + 1), i).wait_send()

        p_y(at_z(Z // 2), 2).wait_send()
        for o in range(1, Y):
            q_y(o).wait_send()
        for o in range(Y):
            for hop in range(HOPS):
                q_up(z, o, hop).wait_send()
                q_down(z, o, hop).wait_send()
            last_hop(o)(z, o, HOPS).wait_send()

    def p_ring(distance):
        if distance > HOPS:
            zz = at_z(distance)
            for i in range(2):
                p_turn(zz, i).wait_recv()
            p_spread(zz, True)
            return
        for i, (send, zz) in enumerate(((p_up, at_z(-distance)), (p_down, at_z(distance)))):
            send(zz, 0).wait_recv()
            if distance < HOPS:
                send(zz, distance).start()
            else:
                p_turn(zz, i).start()
            p_spread(zz, False)

    def p_pass(distance):
        for zz in both(distance):
            for i in range(2):
                p_y_in(zz, i).wait_recv()
                if distance <= HOPS:
                    p_far(zz, i).start()

    def p_end(distance):
        for zz in both(distance):
            if distance <= HOPS:
                for i in range(2):
                    p_far_in(zz, i).wait_recv()
            else:
                p_y_in(zz, 2).wait_recv()

    def q_first():
        for o in (1, 3, 2):
            q_y_in(o).wait_recv()
            q_up(z, o, 0).start()
            q_down(z, o, 0).start()

    def q_ring(distance, others):
        for o in others:
            for send, zz in ((q_up, at_z(-distance)), (q_down, at_z(distance))):
                if distance <= HOPS or send is last_hop(o):
                    send(zz, o, 0).wait_recv()
                if distance < HOPS or (distance == HOPS and send is last_hop(o)):
                    send(zz, o, distance).start()

    own, rest = (0,), (1, 3, 2)

    loads[1].wait()
    loads[2].wait()
    step = INNER // 4
    low = jnp.zeros((ROWS, RANK), F32)
    for i in range(4):
        cols = pl.ds(i * step, step)
        low = low + nt(inner[:, cols], narrow[:, cols])
    low = low.astype(BF16)

    loads[3].wait()
    loads[4].wait()
    loads[5].wait()
    loads[6].wait()
    trailing = trunk[...].astype(F32) + nn(low, widen[...])
    centred = trailing - jnp.mean(trailing, axis=1, keepdims=True)
    inv_std = lax.rsqrt(jnp.mean(centred * centred, axis=1, keepdims=True) + norm_eps)
    spread = centred * inv_std
    normed[...] = spread
    head_in = (spread * gain[...] + bias[...]).astype(BF16)
    p_ring(1)
    p_pass(0)
    q_ring(1, own)
    q_first()
    loads[7].wait()
    embedding = nn(head_in, head[...])
    inv_len = lax.rsqrt(jnp.sum(embedding * embedding, axis=1, keepdims=True) + norm_eps)
    embedding = embedding * inv_len
    unit[...] = embedding

    half = E // 2

    def to_wire(ref, value):
        ref[...] = jnp.concatenate([value[:, :half], value[:, half:]], axis=0).astype(BF16)

    def from_wire(ref):
        value = ref[...].astype(F32)
        return jnp.concatenate([value[:ROWS], value[ROWS:]], axis=1)

    to_wire(image_wire.at[c, x], embedding)

    def send_images(o):
        ref = image_wire.at[c, x]
        return remote(ref, ref, img_send.at[o - 1], img_recv.at[x], device(at_x(o), y, z, c))

    def images_over(xx):
        ref = image_wire.at[c, xx]
        return remote(ref, ref, over_send.at[xx], over_recv.at[xx], sibling)

    @pl.loop(1, X)
    def _(o):
        send_images(o).start()

    images_over(x).start()

    @pending.append
    def _():
        @pl.loop(1, X)
        def _(o):
            send_images(o).wait_send()

        @pl.loop(0, X)
        def _(xx):
            images_over(xx).wait_send()

    p_ring(2)
    p_pass(1)
    q_ring(1, rest)
    q_ring(2, own)
    p_ring(3)
    p_pass(2)
    q_ring(2, rest)
    q_ring(3, own)
    p_end(0)

    @pl.loop(1, X)
    def _(o):
        ref = image_wire.at[c, at_x(o)]
        remote(ref, ref, img_send.at[0], img_recv.at[at_x(o)], sibling).wait_recv()
        images_over(at_x(o)).start()

    p_ring(4)
    p_pass(3)

    @pl.loop(0, X)
    def _(xx):
        ref = image_wire.at[1 - c, xx]
        remote(ref, ref, over_send.at[0], over_recv.at[xx], sibling).wait_recv()

    for i in range(0, 2 * X, 2):
        two = [from_wire(image_wire.at[j // X, j % X]) for j in (i, i + 1)]
        images[pl.ds(i * ROWS, 2 * ROWS)] = jnp.concatenate(two, axis=0).astype(BF16)

    loads[8].wait()
    loads[9].wait()
    sharp = jnp.exp(jnp.full((1, 2 * TEXTS), sharp_s[0], F32))
    shift = jnp.full((1, 2 * TEXTS), shift_s[0], F32)
    dv[...] = jnp.zeros_like(dv)

    q_ring(3, rest)

    def fill(i, zz):
        part = pl.ds(i * TEXTS, TEXTS)
        tile[part, :PC] = tp[c, zz].astype(F32).reshape(TEXTS, PC).astype(BF16)
        tile[part, PC:] = tq[c, zz].astype(F32).reshape(TEXTS, QC).astype(BF16)

    @pl.loop(0, Z // 2)
    def _(s):
        @pl.when(s == 1)
        def _():
            p_end(1)

        @pl.when(s == 2)
        def _():
            p_end(2)

        @pl.when(s == 3)
        def _():
            p_end(3)

        fill(0, at_z(-s))

        @pl.when(s == 0)
        def _():
            tile[pl.ds(TEXTS, TEXTS)] = jnp.zeros((TEXTS, E), BF16)

        @pl.when(s > 0)
        def _():
            fill(1, at_z(s))

        cosine = nt(images[...], tile[...])
        row = lax.broadcasted_iota(jnp.int32, cosine.shape, 0) - (c * X + x) * ROWS
        col = lax.broadcasted_iota(jnp.int32, cosine.shape, 1) - y * ROWS
        same = (row == col) & (row >= 0) & (row < ROWS) & (s == 0)
        weights = sharp * (jax.nn.sigmoid(sharp * cosine + shift) - jnp.where(same, 1.0, 0.0))
        dv[...] += nn(weights.astype(BF16), tile[...])

    def send_sum(o):
        return remote(
            dv_send.at[o - 1],
            dv_recv.at[x],
            rs_send.at[o - 1],
            rs_recv.at[x],
            device(at_x(o), y, z, c),
        )

    def cross(o):
        return remote(
            cross_send.at[o], cross_recv.at[o], cross_ssem.at[o], cross_rsem.at[o], sibling
        )

    def rows_of(core, xx):
        return pl.ds(pl.multiple_of((core * X + xx) * ROWS, 8), ROWS)

    order = (2, 1, 3, 0)
    q_ring(4, own + rest)
    p_pass(4)
    p_end(4)
    fill(0, at_z(Z // 2))
    last = pl.ds(0, TEXTS)
    for core in (1 - c, c):
        rows = pl.ds(pl.multiple_of(core * SIDE, SIDE), SIDE)
        cosine = nt(images[rows], tile[last])
        weights = sharp[:, :TEXTS] * jax.nn.sigmoid(sharp[:, :TEXTS] * cosine + shift[:, :TEXTS])
        dv[rows] += nn(weights.astype(BF16), tile[last])
        if core is not c:
            for o in order:
                to_wire(cross_send.at[o], dv[rows_of(1 - c, at_x(o))])
                cross(o).start()
    for o in order:
        cross(o).wait_recv()
        derivative = dv[rows_of(c, at_x(o))] + from_wire(cross_recv.at[o])
        if o > 0:
            to_wire(dv_send.at[o - 1], derivative)
            send_sum(o).start()

    @pending.append
    def _():
        for o in range(X):
            cross(o).wait_send()
            if o > 0:
                send_sum(o).wait_send()

    for o in (1, 3, 2):
        ref = dv_recv.at[at_x(o)]
        remote(ref, ref, rs_send.at[0], rs_recv.at[at_x(o)], sibling).wait_recv()
        derivative = derivative + from_wire(ref)
    dv_own[...] = derivative
    dv_copy = pltpu.make_async_copy(dv_own, dv_h, out_sem.at[0])
    dv_copy.start()
    pending.append(dv_copy.wait)

    embedding = unit[...]
    along = jnp.sum(embedding * derivative, axis=1, keepdims=True)
    embed_grad = (inv_len * (derivative - embedding * along)).astype(BF16)
    scaled = nt(embed_grad, head[...]) * gain[...]
    spread = normed[...]
    section_grad = inv_std * (
        scaled
        - jnp.mean(scaled, axis=1, keepdims=True)
        - spread * jnp.mean(scaled * spread, axis=1, keepdims=True)
    )
    section_grad = section_grad.astype(BF16)
    section[...] = section_grad
    back = nt(widen[...], section_grad).astype(BF16)

    n_down, n_up = INNER // WIDE // 2, DEPTH // WIDE // 2

    def piece(i, core):
        if i < n_down:
            cols = pl.ds(pl.multiple_of((2 * i + core) * WIDE, WIDE), WIDE)
            return nn(back, inner[:, cols])
        if i < n_down + n_up:
            cols = pl.ds(pl.multiple_of((2 * (i - n_down) + core) * WIDE, WIDE), WIDE)
            dims = (((0,), (0,)), ((), ()))
            return lax.dot_general(low, section[:, cols], dims, preferred_element_type=F32)
        return jnp.zeros((RANK, WIDE), F32)

    def pair_copy(h):
        return remote(pair_send.at[h], pair_recv.at[h], pair_ssem.at[h], pair_rsem.at[h], sibling)

    def plane_copy(h, o):
        kk = at_k(o)
        return remote(
            plane_send.at[h, kk],
            plane_recv.at[h, k],
            plane_ssem.at[h, o - 1],
            plane_rsem.at[h, k],
            plane_device(kk),
        )

    def plane_in(h, o):
        ref = plane_recv.at[h, at_k(o)]
        return remote(ref, ref, plane_ssem.at[0, 0], plane_rsem.at[h, at_k(o)], sibling)

    def ring_copy(h, o):
        ref = ring_recv.at[h, z]
        to = device(x, y, at_z(o), c)
        return remote(ref, ref, ring_ssem.at[h, o - 1], ring_rsem.at[h, z], to)

    def ring_in(h, o):
        ref = ring_recv.at[h, at_z(o)]
        return remote(ref, ref, ring_ssem.at[0, 0], ring_rsem.at[h, at_z(o)], sibling)

    def back_copy(h, o):
        ref = final.at[h, c, k]
        return remote(ref, ref, back_ssem.at[h, o - 1], back_rsem.at[h, k], plane_device(at_k(o)))

    def back_in(h, o):
        ref = final.at[h, c, at_k(o)]
        return remote(ref, ref, back_ssem.at[0, 0], back_rsem.at[h, at_k(o)], sibling)

    def last_copy(h, kk):
        ref = final.at[h, c, kk]
        return remote(ref, ref, last_ssem.at[h, kk], last_rsem.at[h, kk], sibling)

    def last_in(h, kk):
        ref = final.at[h, 1 - c, kk]
        return remote(ref, ref, last_ssem.at[0, 0], last_rsem.at[h, kk], sibling)

    def out_copy(h, core):
        return pltpu.make_async_copy(
            final.at[h, core], grad_h.at[h, core], out_sem.at[1 + 2 * h + core]
        )

    for i in range(PLANE):
        value = piece(i, 1 - c).astype(BF16)
        for h in range(PARTS):
            pair_send[h, i] = value[:, h * CUT : (h + 1) * CUT]
    for h in range(PARTS):
        pair_copy(h).start()
    for i in range(PLANE):
        value = piece(i, c)
        for h in range(PARTS):
            grads[h, i] = value[:, h * CUT : (h + 1) * CUT]
    for h in range(PARTS):
        pair_copy(h).wait_recv()
        plane_send[h] = (grads[h] + pair_recv[h].astype(F32)).astype(BF16)

        @pl.loop(1, PLANE)
        def _(o):
            plane_copy(h, o).start()

        plane_recv[h, k] = plane_send[h, k]
    for h in range(PARTS):

        @pl.loop(1, PLANE)
        def _(o):
            plane_in(h, o).wait_recv()

        ring_recv[h, z] = jnp.sum(plane_recv[h].astype(F32), axis=0).astype(BF16)

        @pl.loop(1, Z)
        def _(o):
            ring_copy(h, o).start()

    for h in range(PARTS):

        @pl.loop(1, Z)
        def _(o):
            ring_in(h, o).wait_recv()

        final[h, c, k] = jnp.sum(ring_recv[h].astype(F32), axis=0).astype(BF16)

        @pl.loop(1, PLANE)
        def _(o):
            back_copy(h, o).start()

        last_copy(h, k).start()
    for h in range(PARTS):

        @pl.loop(1, PLANE)
        def _(o):
            back_in(h, o).wait_recv()
            last_copy(h, at_k(o)).start()

        out_copy(h, c).start()
    for h in range(PARTS):

        @pl.loop(0, PLANE)
        def _(kk):
            last_in(h, kk).wait_recv()

        out_copy(h, 1 - c).start()

    @pending.append
    def _():
        for h in range(PARTS):
            pair_copy(h).wait_send()

            @pl.loop(1, PLANE)
            def _(o):
                plane_copy(h, o).wait_send()
                back_copy(h, o).wait_send()

            @pl.loop(1, Z)
            def _(o):
                ring_copy(h, o).wait_send()

            @pl.loop(0, PLANE)
            def _(kk):
                last_copy(h, kk).wait_send()

            for core in range(2):
                out_copy(h, core).wait()

    for wait in pending:
        wait()


def finish(
    dv_h, grad_h, dv_out, down_out, up_out, dv, pieces, whole, in_sem, dv_sem, down_sem, up_sem
):
    reads = [
        pltpu.make_async_copy(dv_h, dv, in_sem.at[0]),
        pltpu.make_async_copy(grad_h, pieces, in_sem.at[1]),
    ]
    for read in reads:
        read.start()
    for read in reads:
        read.wait()
    dv_copy = pltpu.make_async_copy(dv, dv_out, dv_sem)
    dv_copy.start()

    def out(i):
        if i < INNER // DEPTH:
            cols = pl.ds(i * DEPTH, DEPTH)
            return pltpu.make_async_copy(whole.at[:, cols], down_out.at[:, cols], down_sem.at[i])
        return pltpu.make_async_copy(whole.at[:, pl.ds(INNER, DEPTH)], up_out, up_sem)

    count = (INNER + DEPTH) // DEPTH
    for i in range(count):
        for j in range(i * DEPTH // CUT, (i + 1) * DEPTH // CUT):
            wide = j // PARTS
            piece = pieces[j % PARTS, wide % 2, wide // 2]
            whole[:, pl.ds(j * CUT, CUT)] = piece.astype(F32)
        out(i).start()
    for i in range(count):
        out(i).wait()
    dv_copy.wait()


def body(
    gelu_pooled_inner,
    frozen_pooled_trunk_result,
    narrowing_weight,
    widening_weight,
    closing_standardize_multiplier,
    closing_standardize_addend,
    closing_projection_weight,
    sentence_encodings,
    logged_sharpening,
    sigmoid_threshold_term,
):
    anywhere = pl.BlockSpec(memory_space=pl.ANY)
    dma = pltpu.SemaphoreType.DMA
    derivative, pieces = pl.pallas_call(
        kernel,
        out_shape=(
            jax.ShapeDtypeStruct((ROWS, E), F32),
            jax.ShapeDtypeStruct((PARTS, 2, PLANE, RANK, CUT), BF16),
        ),
        in_specs=[anywhere] * 8 + [pl.BlockSpec(memory_space=pltpu.HBM)] * 2,
        out_specs=(anywhere, anywhere),
        scratch_shapes=[
            pltpu.VMEM((ROWS, INNER), BF16),
            pltpu.VMEM((ROWS, DEPTH), BF16),
            pltpu.VMEM((RANK, INNER), BF16),
            pltpu.VMEM((RANK, DEPTH), BF16),
            pltpu.VMEM((1, DEPTH), F32),
            pltpu.VMEM((1, DEPTH), F32),
            pltpu.VMEM((DEPTH, E), BF16),
            pltpu.VMEM((ROWS, E), BF16),
            pltpu.SMEM((1,), F32),
            pltpu.SMEM((1,), F32),
            pltpu.VMEM((2, Z, Y, ROWS, PC), BF16),
            pltpu.VMEM((2, Z, Y, ROWS, QC), BF16),
            pltpu.VMEM((2 * TEXTS, E), BF16),
            pltpu.VMEM((2, X, 2 * ROWS, E // 2), BF16),
            pltpu.VMEM((IMAGES, E), BF16),
            pltpu.VMEM((IMAGES, E), F32),
            pltpu.VMEM((X, 2 * ROWS, E // 2), BF16),
            pltpu.VMEM((X, 2 * ROWS, E // 2), BF16),
            pltpu.VMEM((X - 1, 2 * ROWS, E // 2), BF16),
            pltpu.VMEM((X, 2 * ROWS, E // 2), BF16),
            pltpu.VMEM((ROWS, E), F32),
            pltpu.VMEM((ROWS, E), F32),
            pltpu.VMEM((ROWS, DEPTH), F32),
            pltpu.VMEM((ROWS, DEPTH), BF16),
            pltpu.VMEM((PARTS, PLANE, RANK, CUT), F32),
            pltpu.VMEM((PARTS, PLANE, RANK, CUT), BF16),
            pltpu.VMEM((PARTS, PLANE, RANK, CUT), BF16),
            pltpu.VMEM((PARTS, PLANE, RANK, CUT), BF16),
            pltpu.VMEM((PARTS, PLANE, RANK, CUT), BF16),
            pltpu.VMEM((PARTS, Z, RANK, CUT), BF16),
            pltpu.VMEM((PARTS, 2, PLANE, RANK, CUT), BF16),
            dma((10,)),
            dma((2 * HOPS,)),
            dma((Z,)),
            dma((2,)),
            dma((2,)),
            dma((Z, 3)),
            dma((Z, 3)),
            dma((Z, 2)),
            dma((Z, 2)),
            dma((Y - 1,)),
            dma((Y,)),
            dma((2 * HOPS + 2, Y)),
            dma((Z, Y)),
            dma((X - 1,)),
            dma((X,)),
            dma((X,)),
            dma((X,)),
            dma((X,)),
            dma((X,)),
            dma((X - 1,)),
            dma((X,)),
            dma((PARTS,)),
            dma((PARTS,)),
            dma((PARTS, PLANE - 1)),
            dma((PARTS, PLANE)),
            dma((PARTS, Z - 1)),
            dma((PARTS, Z)),
            dma((PARTS, PLANE - 1)),
            dma((PARTS, PLANE)),
            dma((PARTS, PLANE)),
            dma((PARTS, PLANE)),
            dma((1 + 2 * PARTS,)),
        ],
        compiler_params=pltpu.CompilerParams(
            collective_id=0, has_side_effects=True, vmem_limit_bytes=64_800_000
        ),
    )(
        gelu_pooled_inner,
        frozen_pooled_trunk_result,
        narrowing_weight.T,
        widening_weight,
        closing_standardize_multiplier.reshape(1, DEPTH),
        closing_standardize_addend.reshape(1, DEPTH),
        closing_projection_weight,
        sentence_encodings,
        logged_sharpening,
        sigmoid_threshold_term,
    )
    derivative, down, up = pl.pallas_call(
        finish,
        out_shape=(
            jax.ShapeDtypeStruct((ROWS, E), F32),
            jax.ShapeDtypeStruct((RANK, INNER), F32),
            jax.ShapeDtypeStruct((RANK, DEPTH), F32),
        ),
        in_specs=[anywhere] * 2,
        out_specs=(anywhere,) * 3,
        scratch_shapes=[
            pltpu.VMEM((ROWS, E), F32),
            pltpu.VMEM((PARTS, 2, PLANE, RANK, CUT), BF16),
            pltpu.VMEM((RANK, INNER + DEPTH), F32),
            dma((2,)),
            dma,
            dma((INNER // DEPTH,)),
            dma,
        ],
        compiler_params=pltpu.CompilerParams(vmem_limit_bytes=64_800_000),
    )(derivative, pieces)
    return derivative, down.T, up


def solution(mesh):
    rows = P(("group", "dp"), None)
    return jax.shard_map(
        body,
        mesh=mesh,
        in_specs=(rows, rows, P(), P(), P(), P(), P(), rows, P(), P()),
        out_specs=(rows, P(), P()),
        check_vma=False,
    )
```

```python
import jax
import jax.numpy as jnp
from jax import lax
from jax.experimental import pallas as pl
from jax.experimental.pallas import tpu as pltpu
from jax.sharding import PartitionSpec as P

norm_eps = 1e-06
MESH = pl.DeviceIdType.MESH
BF16, F32 = jnp.bfloat16, jnp.float32

X, YL, YH, Z = 4, 2, 2, 8
Y = YL * YH
ROWS = 56
E, DEPTH, INNER, RANK = 1024, 3072, 12288, 16
PC = 640
QC = E - PC
FORE = 256
SIDE = X * ROWS
IMAGES = 2 * SIDE
TEXTS = Y * ROWS
PLANE = X * Y
WIDE = 512
PARTS = 2
CUT = WIDE // PARTS
HOPS = Z // 2 - 1


def remote(src, dst, send_sem, recv_sem, device):
    return pltpu.make_async_remote_copy(
        src_ref=src,
        dst_ref=dst,
        send_sem=send_sem,
        recv_sem=recv_sem,
        device_id=device,
        device_id_type=MESH,
    )


def nt(a, b):
    return lax.dot_general(a, b, (((1,), (1,)), ((), ())), preferred_element_type=F32)


def nn(a, b):
    return lax.dot_general(a, b, (((1,), (0,)), ((), ())), preferred_element_type=F32)


def kernel(
    inner_h,
    trunk_h,
    narrow_h,
    widen_h,
    gain_h,
    bias_h,
    head_h,
    text_h,
    sharp_h,
    shift_h,
    dv_h,
    grad_h,
    inner,
    trunk,
    narrow,
    widen,
    gain,
    bias,
    head,
    text,
    sharp_s,
    shift_s,
    tp,
    tq,
    tile,
    image_wire,
    images,
    dv,
    cross_send,
    cross_recv,
    dv_send,
    dv_recv,
    dv_own,
    unit,
    normed,
    section,
    grads,
    pair_send,
    pair_recv,
    plane_send,
    plane_recv,
    ring_recv,
    final,
    load_sem,
    pz_send,
    pz_recv,
    pt_send,
    pt_recv,
    py_send,
    py_recv,
    pf_send,
    pf_recv,
    qy_send,
    qy_recv,
    qz_send,
    qz_recv,
    img_send,
    img_recv,
    over_send,
    over_recv,
    cross_ssem,
    cross_rsem,
    rs_send,
    rs_recv,
    pair_ssem,
    pair_rsem,
    plane_ssem,
    plane_rsem,
    ring_ssem,
    ring_rsem,
    back_ssem,
    back_rsem,
    last_ssem,
    last_rsem,
    out_sem,
):
    g, d = lax.axis_index("group"), lax.axis_index("dp")
    c, yh = lax.rem(g, 2), lax.div(g, 2)
    z, yl, x = lax.div(d, YL * X), lax.rem(lax.div(d, X), YL), lax.rem(d, X)
    y = yh * YL + yl
    k = y * X + x

    def device(xx, yy, zz, cc):
        return (
            lax.div(yy, YL) * 2 + cc,
            zz * (YL * X) + lax.rem(yy, YL) * X + xx,
        )

    sibling = device(x, y, z, 1 - c)
    above = device(x, y, lax.rem(z + 1, Z), c)
    below = device(x, y, lax.rem(z + Z - 1, Z), c)

    def at_y(o):
        return lax.rem(y + o, Y)

    def at_x(o):
        return lax.rem(x + o, X)

    def at_z(o):
        return lax.rem(z + o + Z, Z)

    def at_k(o):
        return lax.rem(k + o, PLANE)

    def plane_device(kk):
        return device(lax.rem(kk, X), lax.div(kk, X), z, c)

    loads = [
        pltpu.make_async_copy(text_h, text, load_sem.at[0]),
        pltpu.make_async_copy(inner_h, inner, load_sem.at[1]),
        pltpu.make_async_copy(narrow_h, narrow, load_sem.at[2]),
        pltpu.make_async_copy(widen_h, widen, load_sem.at[3]),
        pltpu.make_async_copy(trunk_h, trunk, load_sem.at[4]),
        pltpu.make_async_copy(gain_h, gain, load_sem.at[5]),
        pltpu.make_async_copy(bias_h, bias, load_sem.at[6]),
        pltpu.make_async_copy(head_h, head, load_sem.at[7]),
        pltpu.make_async_copy(sharp_h, sharp_s, load_sem.at[8]),
        pltpu.make_async_copy(shift_h, shift_s, load_sem.at[9]),
    ]
    loads[0].start()
    barrier = pltpu.get_barrier_semaphore()
    pl.semaphore_signal(barrier, inc=1, device_id=sibling, device_id_type=MESH)

    for neighbour in (above, below):
        pl.semaphore_signal(barrier, inc=1, device_id=neighbour, device_id_type=MESH)
    for o in range(1, Y):
        pl.semaphore_signal(
            barrier, inc=1, device_id=device(x, at_y(o), z, c), device_id_type=MESH
        )
    for o in range(1, X):
        pl.semaphore_signal(
            barrier, inc=1, device_id=device(at_x(o), y, z, c), device_id_type=MESH
        )

    for load in loads[1:]:
        load.start()
    pending = []

    loads[0].wait()
    rows = text[...].astype(F32)
    rows = rows * lax.rsqrt(jnp.sum(rows * rows, axis=1, keepdims=True) + norm_eps)
    tp[c, z, y] = rows[:, :PC].astype(BF16)
    tq[c, z, y] = rows[:, PC:].astype(BF16)

    pl.semaphore_wait(barrier, 1 + 2 + (Y - 1) + (X - 1))

    def p_up(zz, hop):
        ref = tp.at[c, zz, y]
        return remote(ref, ref, pz_send.at[hop], pz_recv.at[zz], above)

    def p_down(zz, hop):
        ref = tp.at[c, zz, y]
        return remote(ref, ref, pz_send.at[HOPS + hop], pz_recv.at[zz], below)

    def half_of(ref, i):
        return ref.at[:, pl.ds((0, FORE)[i], (FORE, PC - FORE)[i])]

    def p_turn(zz, i):
        ref = half_of(tp.at[c, zz, y], i)
        return remote(ref, ref, pt_send.at[i], pt_recv.at[i], (above, below)[i])

    def p_y(zz, i):
        ref = tp.at[c, zz, y]
        to = device(x, at_y((1, Y - 1, 2)[i]), z, c)
        return remote(ref, ref, py_send.at[zz, i], py_recv.at[zz, i], to)

    def p_y_in(zz, i):
        ref = tp.at[c, zz, at_y((Y - 1, 1, 2)[i])]
        return remote(ref, ref, py_send.at[0, 0], py_recv.at[zz, i], sibling)

    def p_far(zz, i):
        ref = half_of(tp.at[c, zz, at_y((Y - 1, 1)[i])], i)
        to = device(x, at_y((1, Y - 1)[i]), z, c)
        return remote(ref, ref, pf_send.at[zz, i], pf_recv.at[zz, i], to)

    def p_far_in(zz, i):
        ref = half_of(tp.at[c, zz, at_y(2)], i)
        return remote(ref, ref, pf_send.at[0, 0], pf_recv.at[zz, i], sibling)

    def q_y(o):
        ref = tq.at[c, z, y]
        return remote(ref, ref, qy_send.at[o - 1], qy_recv.at[y], device(x, at_y(o), z, c))

    def q_y_in(o):
        ref = tq.at[c, z, at_y(o)]
        return remote(ref, ref, qy_send.at[0], qy_recv.at[at_y(o)], sibling)

    def q_up(zz, o, hop):
        ref = tq.at[c, zz, at_y(o)]
        return remote(ref, ref, qz_send.at[hop, o], qz_recv.at[zz, at_y(o)], above)

    def q_down(zz, o, hop):
        ref = tq.at[c, zz, at_y(o)]
        return remote(ref, ref, qz_send.at[HOPS + 1 + hop, o], qz_recv.at[zz, at_y(o)], below)

    def both(distance):
        if distance in (0, Z // 2):
            return [at_z(distance)]
        return [at_z(-distance), at_z(distance)]

    def p_spread(zz, whole):
        for i in range(2 + whole):
            p_y(zz, i).start()

    p_up(z, 0).start()
    p_down(z, 0).start()
    p_spread(z, False)
    for o in (2, 1, 3):
        q_y(o).start()
    q_up(z, 0, 0).start()
    q_down(z, 0, 0).start()

    def last_hop(o):
        return (q_up, q_down)[o % 2]

    @pending.append
    def _():
        for hop in range(HOPS):
            p_up(z, hop).wait_send()
            p_down(z, hop).wait_send()
        for i in range(2):
            p_turn(z, i).wait_send()

        @pl.loop(0, Z)
        def _(zz):
            for i in range(2):
                p_y(zz, i).wait_send()

        @pl.loop(0, Z - 1)
        def _(zz):
            for i in range(2):
                p_far(at_z(zz + Z // 2 + 1), i).wait_send()

        p_y(at_z(Z // 2), 2).wait_send()
        for o in range(1, Y):
            q_y(o).wait_send()
        for o in range(Y):
            for hop in range(HOPS):
                q_up(z, o, hop).wait_send()
                q_down(z, o, hop).wait_send()
            last_hop(o)(z, o, HOPS).wait_send()

    def p_ring(distance):
        if distance > HOPS:
            zz = at_z(distance)
            for i in range(2):
                p_turn(zz, i).wait_recv()
            p_spread(zz, True)
            return
        for i, (send, zz) in enumerate(((p_up, at_z(-distance)), (p_down, at_z(distance)))):
            send(zz, 0).wait_recv()
            if distance < HOPS:
                send(zz, distance).start()
            else:
                p_turn(zz, i).start()
            p_spread(zz, False)

    def p_pass(distance):
        for zz in both(distance):
            for i in range(2):
                p_y_in(zz, i).wait_recv()
                if distance <= HOPS:
                    p_far(zz, i).start()

    def p_end(distance):
        for zz in both(distance):
            if distance <= HOPS:
                for i in range(2):
                    p_far_in(zz, i).wait_recv()
            else:
                p_y_in(zz, 2).wait_recv()

    def q_first():
        for o in (1, 3, 2):
            q_y_in(o).wait_recv()
            q_up(z, o, 0).start()
            q_down(z, o, 0).start()

    def q_ring(distance, others):
        for o in others:
            for send, zz in ((q_up, at_z(-distance)), (q_down, at_z(distance))):
                if distance <= HOPS or send is last_hop(o):
                    send(zz, o, 0).wait_recv()
                if distance < HOPS or (distance == HOPS and send is last_hop(o)):
                    send(zz, o, distance).start()

    own, rest = (0,), (1, 3, 2)

    loads[1].wait()
    loads[2].wait()
    step = INNER // 4
    low = jnp.zeros((ROWS, RANK), F32)
    for i in range(4):
        cols = pl.ds(i * step, step)
        low = low + nt(inner[:, cols], narrow[:, cols])
    low = low.astype(BF16)

    loads[3].wait()
    loads[4].wait()
    loads[5].wait()
    loads[6].wait()
    trailing = trunk[...].astype(F32) + nn(low, widen[...])
    centred = trailing - jnp.mean(trailing, axis=1, keepdims=True)
    inv_std = lax.rsqrt(jnp.mean(centred * centred, axis=1, keepdims=True) + norm_eps)
    spread = centred * inv_std
    normed[...] = spread
    head_in = (spread * gain[...] + bias[...]).astype(BF16)
    p_ring(1)
    p_pass(0)
    q_ring(1, own)
    q_first()
    loads[7].wait()
    embedding = nn(head_in, head[...])
    inv_len = lax.rsqrt(jnp.sum(embedding * embedding, axis=1, keepdims=True) + norm_eps)
    embedding = embedding * inv_len
    unit[...] = embedding

    half = E // 2

    def to_wire(ref, value):
        ref[...] = jnp.concatenate([value[:, :half], value[:, half:]], axis=0).astype(BF16)

    def from_wire(ref):
        value = ref[...].astype(F32)
        return jnp.concatenate([value[:ROWS], value[ROWS:]], axis=1)

    to_wire(image_wire.at[c, x], embedding)

    def send_images(o):
        ref = image_wire.at[c, x]
        return remote(ref, ref, img_send.at[o - 1], img_recv.at[x], device(at_x(o), y, z, c))

    def images_over(xx):
        ref = image_wire.at[c, xx]
        return remote(ref, ref, over_send.at[xx], over_recv.at[xx], sibling)

    @pl.loop(1, X)
    def _(o):
        send_images(o).start()

    images_over(x).start()

    @pending.append
    def _():
        @pl.loop(1, X)
        def _(o):
            send_images(o).wait_send()

        @pl.loop(0, X)
        def _(xx):
            images_over(xx).wait_send()

    p_ring(2)
    p_pass(1)
    q_ring(1, rest)
    q_ring(2, own)
    p_ring(3)
    p_pass(2)
    q_ring(2, rest)
    q_ring(3, own)
    p_end(0)

    @pl.loop(1, X)
    def _(o):
        ref = image_wire.at[c, at_x(o)]
        remote(ref, ref, img_send.at[0], img_recv.at[at_x(o)], sibling).wait_recv()
        images_over(at_x(o)).start()

    p_ring(4)
    p_pass(3)

    @pl.loop(0, X)
    def _(xx):
        ref = image_wire.at[1 - c, xx]
        remote(ref, ref, over_send.at[0], over_recv.at[xx], sibling).wait_recv()

    for i in range(0, 2 * X, 2):
        two = [from_wire(image_wire.at[j // X, j % X]) for j in (i, i + 1)]
        images[pl.ds(i * ROWS, 2 * ROWS)] = jnp.concatenate(two, axis=0).astype(BF16)

    loads[8].wait()
    loads[9].wait()
    sharp = jnp.exp(jnp.full((1, 2 * TEXTS), sharp_s[0], F32))
    shift = jnp.full((1, 2 * TEXTS), shift_s[0], F32)
    dv[...] = jnp.zeros_like(dv)

    q_ring(3, rest)

    def fill(i, zz):
        part = pl.ds(i * TEXTS, TEXTS)
        tile[part, :PC] = tp[c, zz].astype(F32).reshape(TEXTS, PC).astype(BF16)
        tile[part, PC:] = tq[c, zz].astype(F32).reshape(TEXTS, QC).astype(BF16)

    @pl.loop(0, Z // 2)
    def _(s):
        @pl.when(s == 1)
        def _():
            p_end(1)

        @pl.when(s == 2)
        def _():
            p_end(2)

        @pl.when(s == 3)
        def _():
            p_end(3)

        fill(0, at_z(-s))

        @pl.when(s == 0)
        def _():
            tile[pl.ds(TEXTS, TEXTS)] = jnp.zeros((TEXTS, E), BF16)

        @pl.when(s > 0)
        def _():
            fill(1, at_z(s))

        cosine = nt(images[...], tile[...])
        row = lax.broadcasted_iota(jnp.int32, cosine.shape, 0) - (c * X + x) * ROWS
        col = lax.broadcasted_iota(jnp.int32, cosine.shape, 1) - y * ROWS
        same = (row == col) & (row >= 0) & (row < ROWS) & (s == 0)
        weights = sharp * (jax.nn.sigmoid(sharp * cosine + shift) - jnp.where(same, 1.0, 0.0))
        dv[...] += nn(weights.astype(BF16), tile[...])

    def send_sum(o):
        return remote(
            dv_send.at[o - 1],
            dv_recv.at[x],
            rs_send.at[o - 1],
            rs_recv.at[x],
            device(at_x(o), y, z, c),
        )

    def cross(o):
        return remote(
            cross_send.at[o], cross_recv.at[o], cross_ssem.at[o], cross_rsem.at[o], sibling
        )

    def rows_of(core, xx):
        return pl.ds(pl.multiple_of((core * X + xx) * ROWS, 8), ROWS)

    order = (2, 1, 3, 0)
    q_ring(4, own + rest)
    p_pass(4)
    p_end(4)
    fill(0, at_z(Z // 2))
    last = pl.ds(0, TEXTS)
    for core in (1 - c, c):
        rows = pl.ds(pl.multiple_of(core * SIDE, SIDE), SIDE)
        cosine = nt(images[rows], tile[last])
        weights = sharp[:, :TEXTS] * jax.nn.sigmoid(sharp[:, :TEXTS] * cosine + shift[:, :TEXTS])
        dv[rows] += nn(weights.astype(BF16), tile[last])
        if core is not c:
            for o in order:
                to_wire(cross_send.at[o], dv[rows_of(1 - c, at_x(o))])
                cross(o).start()
    for o in order:
        cross(o).wait_recv()
        derivative = dv[rows_of(c, at_x(o))] + from_wire(cross_recv.at[o])
        if o > 0:
            to_wire(dv_send.at[o - 1], derivative)
            send_sum(o).start()

    @pending.append
    def _():
        for o in range(X):
            cross(o).wait_send()
            if o > 0:
                send_sum(o).wait_send()

    for o in (1, 3, 2):
        ref = dv_recv.at[at_x(o)]
        remote(ref, ref, rs_send.at[0], rs_recv.at[at_x(o)], sibling).wait_recv()
        derivative = derivative + from_wire(ref)
    dv_own[...] = derivative
    dv_copy = pltpu.make_async_copy(dv_own, dv_h, out_sem.at[0])
    dv_copy.start()
    pending.append(dv_copy.wait)

    embedding = unit[...]
    along = jnp.sum(embedding * derivative, axis=1, keepdims=True)
    embed_grad = (inv_len * (derivative - embedding * along)).astype(BF16)
    scaled = nt(embed_grad, head[...]) * gain[...]
    spread = normed[...]
    section_grad = inv_std * (
        scaled
        - jnp.mean(scaled, axis=1, keepdims=True)
        - spread * jnp.mean(scaled * spread, axis=1, keepdims=True)
    )
    section_grad = section_grad.astype(BF16)
    section[...] = section_grad
    back = nt(widen[...], section_grad).astype(BF16)

    n_down, n_up = INNER // WIDE // 2, DEPTH // WIDE // 2

    def piece(i, core):
        if i < n_down:
            cols = pl.ds(pl.multiple_of((2 * i + core) * WIDE, WIDE), WIDE)
            return nn(back, inner[:, cols])
        if i < n_down + n_up:
            cols = pl.ds(pl.multiple_of((2 * (i - n_down) + core) * WIDE, WIDE), WIDE)
            dims = (((0,), (0,)), ((), ()))
            return lax.dot_general(low, section[:, cols], dims, preferred_element_type=F32)
        return jnp.zeros((RANK, WIDE), F32)

    def pair_copy(h):
        return remote(pair_send.at[h], pair_recv.at[h], pair_ssem.at[h], pair_rsem.at[h], sibling)

    def plane_copy(h, o):
        kk = at_k(o)
        return remote(
            plane_send.at[h, kk],
            plane_recv.at[h, k],
            plane_ssem.at[h, o - 1],
            plane_rsem.at[h, k],
            plane_device(kk),
        )

    def plane_in(h, o):
        ref = plane_recv.at[h, at_k(o)]
        return remote(ref, ref, plane_ssem.at[0, 0], plane_rsem.at[h, at_k(o)], sibling)

    def ring_copy(h, o):
        ref = ring_recv.at[h, z]
        to = device(x, y, at_z(o), c)
        return remote(ref, ref, ring_ssem.at[h, o - 1], ring_rsem.at[h, z], to)

    def ring_in(h, o):
        ref = ring_recv.at[h, at_z(o)]
        return remote(ref, ref, ring_ssem.at[0, 0], ring_rsem.at[h, at_z(o)], sibling)

    def back_copy(h, o):
        ref = final.at[h, c, k]
        return remote(ref, ref, back_ssem.at[h, o - 1], back_rsem.at[h, k], plane_device(at_k(o)))

    def back_in(h, o):
        ref = final.at[h, c, at_k(o)]
        return remote(ref, ref, back_ssem.at[0, 0], back_rsem.at[h, at_k(o)], sibling)

    def last_copy(h, kk):
        ref = final.at[h, c, kk]
        return remote(ref, ref, last_ssem.at[h, kk], last_rsem.at[h, kk], sibling)

    def last_in(h, kk):
        ref = final.at[h, 1 - c, kk]
        return remote(ref, ref, last_ssem.at[0, 0], last_rsem.at[h, kk], sibling)

    def out_copy(h, core):
        return pltpu.make_async_copy(
            final.at[h, core], grad_h.at[h, core], out_sem.at[1 + 2 * h + core]
        )

    for i in range(PLANE):
        value = piece(i, 1 - c).astype(BF16)
        for h in range(PARTS):
            pair_send[h, i] = value[:, h * CUT : (h + 1) * CUT]
    for h in range(PARTS):
        pair_copy(h).start()
    for i in range(PLANE):
        value = piece(i, c)
        for h in range(PARTS):
            grads[h, i] = value[:, h * CUT : (h + 1) * CUT]
    for h in range(PARTS):
        pair_copy(h).wait_recv()
        plane_send[h] = (grads[h] + pair_recv[h].astype(F32)).astype(BF16)

        @pl.loop(1, PLANE)
        def _(o):
            plane_copy(h, o).start()

        plane_recv[h, k] = plane_send[h, k]
    for h in range(PARTS):

        @pl.loop(1, PLANE)
        def _(o):
            plane_in(h, o).wait_recv()

        ring_recv[h, z] = jnp.sum(plane_recv[h].astype(F32), axis=0).astype(BF16)

        @pl.loop(1, Z)
        def _(o):
            ring_copy(h, o).start()

    for h in range(PARTS):

        @pl.loop(1, Z)
        def _(o):
            ring_in(h, o).wait_recv()

        final[h, c, k] = jnp.sum(ring_recv[h].astype(F32), axis=0).astype(BF16)

        @pl.loop(1, PLANE)
        def _(o):
            back_copy(h, o).start()

        last_copy(h, k).start()
    for h in range(PARTS):

        @pl.loop(1, PLANE)
        def _(o):
            back_in(h, o).wait_recv()
            last_copy(h, at_k(o)).start()

        out_copy(h, c).start()
    for h in range(PARTS):

        @pl.loop(0, PLANE)
        def _(kk):
            last_in(h, kk).wait_recv()

        out_copy(h, 1 - c).start()

    @pending.append
    def _():
        for h in range(PARTS):
            pair_copy(h).wait_send()

            @pl.loop(1, PLANE)
            def _(o):
                plane_copy(h, o).wait_send()
                back_copy(h, o).wait_send()

            @pl.loop(1, Z)
            def _(o):
                ring_copy(h, o).wait_send()

            @pl.loop(0, PLANE)
            def _(kk):
                last_copy(h, kk).wait_send()

            for core in range(2):
                out_copy(h, core).wait()

    for wait in pending:
        wait()


def finish(
    dv_h, grad_h, dv_out, down_out, up_out, dv, pieces, whole, in_sem, dv_sem, down_sem, up_sem
):
    count = (INNER + DEPTH) // DEPTH
    slots = DEPTH // WIDE // 2

    def read(i):
        part = pl.ds(i * slots, slots)
        return pltpu.make_async_copy(
            grad_h.at[:, :, part], pieces.at[:, :, part], in_sem.at[1 + i]
        )

    dv_read = pltpu.make_async_copy(dv_h, dv, in_sem.at[0])
    for i in range(count):
        read(i).start()
    dv_read.start()

    def out(i):
        if i < INNER // DEPTH:
            cols = pl.ds(i * DEPTH, DEPTH)
            return pltpu.make_async_copy(whole.at[:, cols], down_out.at[:, cols], down_sem.at[i])
        return pltpu.make_async_copy(whole.at[:, pl.ds(INNER, DEPTH)], up_out, up_sem)

    for i in range(count):
        read(i).wait()
        for j in range(i * DEPTH // CUT, (i + 1) * DEPTH // CUT):
            wide = j // PARTS
            piece = pieces[j % PARTS, wide % 2, wide // 2]
            whole[:, pl.ds(j * CUT, CUT)] = piece.astype(F32)
        out(i).start()
    dv_read.wait()
    dv_copy = pltpu.make_async_copy(dv, dv_out, dv_sem)
    dv_copy.start()
    for i in range(count):
        out(i).wait()
    dv_copy.wait()


def body(
    gelu_pooled_inner,
    frozen_pooled_trunk_result,
    narrowing_weight,
    widening_weight,
    closing_standardize_multiplier,
    closing_standardize_addend,
    closing_projection_weight,
    sentence_encodings,
    logged_sharpening,
    sigmoid_threshold_term,
):
    anywhere = pl.BlockSpec(memory_space=pl.ANY)
    dma = pltpu.SemaphoreType.DMA
    derivative, pieces = pl.pallas_call(
        kernel,
        out_shape=(
            jax.ShapeDtypeStruct((ROWS, E), F32),
            jax.ShapeDtypeStruct((PARTS, 2, PLANE, RANK, CUT), BF16),
        ),
        in_specs=[anywhere] * 8 + [pl.BlockSpec(memory_space=pltpu.HBM)] * 2,
        out_specs=(anywhere, anywhere),
        scratch_shapes=[
            pltpu.VMEM((ROWS, INNER), BF16),
            pltpu.VMEM((ROWS, DEPTH), BF16),
            pltpu.VMEM((RANK, INNER), BF16),
            pltpu.VMEM((RANK, DEPTH), BF16),
            pltpu.VMEM((1, DEPTH), F32),
            pltpu.VMEM((1, DEPTH), F32),
            pltpu.VMEM((DEPTH, E), BF16),
            pltpu.VMEM((ROWS, E), BF16),
            pltpu.SMEM((1,), F32),
            pltpu.SMEM((1,), F32),
            pltpu.VMEM((2, Z, Y, ROWS, PC), BF16),
            pltpu.VMEM((2, Z, Y, ROWS, QC), BF16),
            pltpu.VMEM((2 * TEXTS, E), BF16),
            pltpu.VMEM((2, X, 2 * ROWS, E // 2), BF16),
            pltpu.VMEM((IMAGES, E), BF16),
            pltpu.VMEM((IMAGES, E), F32),
            pltpu.VMEM((X, 2 * ROWS, E // 2), BF16),
            pltpu.VMEM((X, 2 * ROWS, E // 2), BF16),
            pltpu.VMEM((X - 1, 2 * ROWS, E // 2), BF16),
            pltpu.VMEM((X, 2 * ROWS, E // 2), BF16),
            pltpu.VMEM((ROWS, E), F32),
            pltpu.VMEM((ROWS, E), F32),
            pltpu.VMEM((ROWS, DEPTH), F32),
            pltpu.VMEM((ROWS, DEPTH), BF16),
            pltpu.VMEM((PARTS, PLANE, RANK, CUT), F32),
            pltpu.VMEM((PARTS, PLANE, RANK, CUT), BF16),
            pltpu.VMEM((PARTS, PLANE, RANK, CUT), BF16),
            pltpu.VMEM((PARTS, PLANE, RANK, CUT), BF16),
            pltpu.VMEM((PARTS, PLANE, RANK, CUT), BF16),
            pltpu.VMEM((PARTS, Z, RANK, CUT), BF16),
            pltpu.VMEM((PARTS, 2, PLANE, RANK, CUT), BF16),
            dma((10,)),
            dma((2 * HOPS,)),
            dma((Z,)),
            dma((2,)),
            dma((2,)),
            dma((Z, 3)),
            dma((Z, 3)),
            dma((Z, 2)),
            dma((Z, 2)),
            dma((Y - 1,)),
            dma((Y,)),
            dma((2 * HOPS + 2, Y)),
            dma((Z, Y)),
            dma((X - 1,)),
            dma((X,)),
            dma((X,)),
            dma((X,)),
            dma((X,)),
            dma((X,)),
            dma((X - 1,)),
            dma((X,)),
            dma((PARTS,)),
            dma((PARTS,)),
            dma((PARTS, PLANE - 1)),
            dma((PARTS, PLANE)),
            dma((PARTS, Z - 1)),
            dma((PARTS, Z)),
            dma((PARTS, PLANE - 1)),
            dma((PARTS, PLANE)),
            dma((PARTS, PLANE)),
            dma((PARTS, PLANE)),
            dma((1 + 2 * PARTS,)),
        ],
        compiler_params=pltpu.CompilerParams(
            collective_id=0, has_side_effects=True, vmem_limit_bytes=64_800_000
        ),
    )(
        gelu_pooled_inner,
        frozen_pooled_trunk_result,
        narrowing_weight.T,
        widening_weight,
        closing_standardize_multiplier.reshape(1, DEPTH),
        closing_standardize_addend.reshape(1, DEPTH),
        closing_projection_weight,
        sentence_encodings,
        logged_sharpening,
        sigmoid_threshold_term,
    )
    derivative, down, up = pl.pallas_call(
        finish,
        out_shape=(
            jax.ShapeDtypeStruct((ROWS, E), F32),
            jax.ShapeDtypeStruct((RANK, INNER), F32),
            jax.ShapeDtypeStruct((RANK, DEPTH), F32),
        ),
        in_specs=[anywhere] * 2,
        out_specs=(anywhere,) * 3,
        scratch_shapes=[
            pltpu.VMEM((ROWS, E), F32),
            pltpu.VMEM((PARTS, 2, PLANE, RANK, CUT), BF16),
            pltpu.VMEM((RANK, INNER + DEPTH), F32),
            dma((1 + (INNER + DEPTH) // DEPTH,)),
            dma,
            dma((INNER // DEPTH,)),
            dma,
        ],
        compiler_params=pltpu.CompilerParams(vmem_limit_bytes=64_800_000),
    )(derivative, pieces)
    return derivative, down.T, up


def solution(mesh):
    rows = P(("group", "dp"), None)
    return jax.shard_map(
        body,
        mesh=mesh,
        in_specs=(rows, rows, P(), P(), P(), P(), P(), rows, P(), P()),
        out_specs=(rows, P(), P()),
        check_vma=False,
    )
```
